512 devices in a mesh: inst: 64 (over y_lo, z, core), tp: 8 (over x, y_hi).
Axes of the slice: x: 4, y: 4 (y_hi: 2, y_lo: 2; y = y_hi * 2 + y_lo), z: 16, core: 2. Of those that a mesh axis runs over, the one named last changes fastest.
Arguments:
- hidden_state: bfloat16 [8192, 6144], P('inst', 'tp'), may hold values from -3000 to 3000
- norm_gain: bfloat16 [6144], P('tp'), may hold values from 0.099609375 to 1.8984375
- kv_weight: bfloat16 [6144, 8, 256], P('tp'), may hold values from -0.078125 to 0.078125
- queries: bfloat16 [8192, 48, 128], P('inst', 'tp'), may hold values from -120 to 120
- pool_keys: bfloat16 [1280, 8, 128, 128], P('inst', 'tp'), may hold values from -6 to 6
- pool_values: bfloat16 [1280, 8, 128, 128], P('inst', 'tp'), may hold values from -6 to 6
- page_table: int32 [8192, 12], P('inst'), may hold values from 0 to 19, as said below
- lengths: int32 [8192], P('inst'), may hold values from 2 to 1536
- move_target: int32 [2048, 1], P('inst'), may hold values from 0 to 63; in each aligned block of 32 rows (0 to 31, 32 to 63, ...) no two rows name the same one
- move_page: int32 [2048], P('inst'), may hold values from 0 to 19
- move_request: int32 [2048], P('inst'), may hold values from 0 to 127
Outputs:
- attention_out: bfloat16 [8192, 6144], P('inst', 'tp')
- new_kv: bfloat16 [8192, 8, 256], P('inst', 'tp')
The draws below stay inside these ranges and needn't reach their ends.
Inputs may be any that keep to these rules, and one draw needn't show every extreme that they name: `page_table`: each row names 12 distinct pages of its instance's pool. `move_target`: the 32 rows of one instance never name the same destination twice.
All inputs are finite; a program needn't handle non-finite values.
Results may differ from the reference program's by a relative error of at most 0.005.
Values may be sent and summed in bfloat16 or wider, within the bound.
No kernel may reach another device: no remote copies, remote signals or barrier semaphores. Data moves between devices by JAX's collectives and lax.ppermute only.
A program may use at most 64 MiB of HBM per device.

```python
import math
import jax
import jax.numpy as jnp
import numpy as np
from jax import lax

D = 6144
QH = 48
KVH = 8
HD = 128
PAGE = 128
MAXP = 12
POOL = 20
REQ = 128
MIG = 32
MIGS = 2048
ROWS = 8192
PAGES = 1280
N_INST = 64


def keys_base(key):
    sample = jax.random.normal(jax.random.fold_in(key, 500), (PAGES, KVH, PAGE, HD), jnp.float32)
    return jnp.clip(sample, -6.0, 6.0)


def table_base(key):
    rank_keys = jax.random.randint(jax.random.fold_in(key, 600), (ROWS, POOL), 0, 1048576)
    rank_keys = rank_keys * POOL + jnp.arange(POOL, dtype=jnp.int32)[None, :]
    ordering = jnp.argsort(rank_keys, axis=1)
    return ordering[:, :MAXP].astype(jnp.int32)


def draw_page_table(key, part):
    shared = table_base(key)
    return shared


def draw_pool_keys(key, part):
    shared = keys_base(key)
    return shared.astype(jnp.bfloat16)


def draw_queries(key, part):
    key = jax.random.fold_in(key, 7)
    values = jnp.clip(2.5 * jax.random.normal(key, (ROWS, QH, HD), jnp.float32), -15.0, 15.0)
    return values.astype(jnp.bfloat16)


def draw_hidden_state(key, part):
    key = jax.random.fold_in(key, 11)
    draw_one = jax.random.fold_in(key, 1)
    draw_two = jax.random.fold_in(key, 2)
    draw_three = jax.random.fold_in(key, 3)
    rising = 3.0 ** (jnp.arange(D, dtype=jnp.float32) / (D - 1))
    base_draw = jnp.clip(jax.random.normal(draw_one, (ROWS, D), jnp.float32), -6.0, 6.0)
    row_scale = jnp.power(10.0, jax.random.uniform(draw_two, (ROWS, 1), jnp.float32, 0.0, 1.0))
    col_scale = jnp.power(10.0, jax.random.uniform(draw_three, (1, D), jnp.float32, 0.0, 1.0))
    return (base_draw * row_scale * col_scale * rising[None, :]).astype(jnp.bfloat16)


def with_ends(array, rng, smallest, high):
    shape = array.shape
    spot = [jax.random.randint(jax.random.fold_in(rng, axis), (), 0, shape[axis]) for axis in range(len(shape))]
    array = array.at[tuple(spot)].set(smallest)
    longest = shape.index(max(shape))
    spot[longest] = (spot[longest] + 1) % shape[longest]
    return array.at[tuple(spot)].set(high)


def block_levels(stream_key, dims, shards, low, largest):
    def one(position, parts):
        heights = jax.random.uniform(jax.random.fold_in(jax.random.fold_in(stream_key, 6), position), (parts,), jnp.float32, low / len(shards), largest / len(shards))
        return jnp.repeat(jnp.exp(heights), dims[position] // parts).reshape((-1,) + (1,) * (len(dims) - position - 1))

    factor_of = one(*shards[0])
    for cut in shards[1:]:
        factor_of = factor_of * one(*cut)
    return factor_of


def routed_block(stream_key, own, number, rows, number_of, top, limit, lean):
    order = jax.random.permutation(stream_key, number_of)
    crowded, ordinary = portions_of(number_of, rows * top, limit, lean, True), portions_of(number_of, rows * top, limit, lean, False)
    places = jnp.arange(number_of)

    def named(tallies, rotation):
        used = int((tallies > 0).sum())
        fixed = max(1, used // 4)
        passed = fixed + (places - fixed + rotation * (used - fixed)) % max(1, number_of - fixed)
        return jnp.zeros((number_of,), jnp.int32).at[order[jnp.where(places < fixed, places, passed)]].set(jnp.asarray(tallies, jnp.int32))

    tallies = jnp.where(number % 4 == 0, named(crowded, number // 4), named(ordinary, number - number // 4 - 1))
    mixed = jax.random.permutation(jax.random.fold_in(own, 3), number_of)
    source_of, taker = mixed[0:number_of // 2 * 2:2], mixed[1:number_of // 2 * 2:2]
    slack = jnp.minimum(tallies[source_of] - 1, limit - tallies[taker]) // 2
    slack = jnp.where((source_of == order[0]) | (taker == order[0]) | (tallies[taker] == 0), 0, jnp.maximum(slack, 0))
    passed = jax.random.randint(jax.random.fold_in(own, 4), (number_of // 2,), 0, 1 << 20) % (slack + 1)
    tallies = tallies.at[source_of].add(-passed).at[taker].add(passed)
    members = jnp.searchsorted(jnp.cumsum(tallies), jnp.arange(rows * top), side="right").astype(jnp.int32)
    table = members.reshape(top, rows).T
    table = table[jax.random.permutation(jax.random.fold_in(own, 1), rows)]
    rotation = jax.random.randint(jax.random.fold_in(own, 2), (rows, 1), 0, top)
    return jnp.take_along_axis(table, (jnp.arange(top)[None, :] + rotation) % top, axis=1)


def portions_of(number_of, total, bound, skew, full):
    loads = [(1 << 20) // math.isqrt(grade ** skew) + 1 for grade in range(1, number_of + 1)]
    largest = bound if full else min(bound, max(-(-total // number_of), total * loads[0] // sum(loads)))
    least = 1 if total - largest >= number_of - 1 else 0
    given, rest = [largest] + [least] * (number_of - 1), total - largest - least * (number_of - 1)
    while rest > 0:
        free = [i for i in range(1, number_of) if given[i] < largest] or [i for i in range(1, number_of) if given[i] < bound]
        whole, budget = sum([loads[i] for i in free]), rest
        for i in free:
            addition = min(bound - given[i], max(1, budget * loads[i] // whole), rest)
            given[i] = given[i] + addition
            rest = rest - addition
    return np.array(given)


def noise(own_key, shape, deviation, bound, shards=(), kind=jnp.bfloat16):
    result = jax.random.normal(own_key, shape, jnp.float32) * deviation
    if len(shards) > 0:
        result = block_levels(own_key, shape, shards, -0.22, 0.18) * result
    return jnp.clip(result, min=-bound, max=bound).astype(kind)


def setup_inputs(seed: int = 0) -> dict:
    key_of = jax.random.split(jax.random.key(seed), 12)
    hidden_state = draw_hidden_state(jax.random.fold_in(key_of[11], 71), 0)
    norm_gain = jnp.clip(1.0 + 0.18 * jax.random.normal(key_of[1], (D,), jnp.float32), 0.099609375, 1.8984375).astype(jnp.bfloat16)
    kv_weight = noise(key_of[2], (D, KVH, 2 * HD), D ** -0.5, 0.078125, ((0, 8),))
    queries = draw_queries(jax.random.fold_in(key_of[11], 71), 0)
    pool_keys = draw_pool_keys(jax.random.fold_in(key_of[11], 71), 0)
    pool_values = noise(key_of[5], (PAGES, KVH, PAGE, HD), 1.0, 6.0, ((0, 64), (1, 8)))
    page_table = draw_page_table(jax.random.fold_in(key_of[11], 71), 0)
    lengths = with_ends(jax.random.randint(key_of[7], (ROWS,), 2, MAXP * PAGE + 1), jax.random.fold_in(key_of[7], 1), 2, MAXP * PAGE).astype(jnp.int32)
    move_target_keys = jax.random.split(jax.random.fold_in(key_of[8], 1), MIGS // MIG)
    move_target_turns = jax.random.permutation(jax.random.fold_in(key_of[8], 3), MIGS // MIG)
    move_target = jax.vmap(lambda own, number: routed_block(jax.random.fold_in(key_of[8], 2), own, number, MIG, N_INST, 1, 1, 2))(move_target_keys, move_target_turns).reshape((MIGS, 1))
    move_page = with_ends(jax.random.randint(key_of[9], (MIGS,), 0, POOL), jax.random.fold_in(key_of[9], 1), 0, POOL - 1).astype(jnp.int32)
    move_request = with_ends(jax.random.randint(key_of[10], (MIGS,), 0, REQ), jax.random.fold_in(key_of[10], 1), 0, REQ - 1).astype(jnp.int32)
    return dict(hidden_state=hidden_state, norm_gain=norm_gain, kv_weight=kv_weight, queries=queries, pool_keys=pool_keys, pool_values=pool_values, page_table=page_table, lengths=lengths, move_target=move_target, move_page=move_page, move_request=move_request)


EPSILON = 1e-05
ROPE_BASE = 1000000.0
FLOOR_SCORE = -1e+30

def rotate_keys(key_rows, positions):
    half_width = key_rows.shape[-1] // 2
    freq_steps = jnp.arange(half_width, dtype=jnp.float32)
    frequency = ROPE_BASE ** (-2.0 * freq_steps / key_rows.shape[-1])
    angles = positions.astype(jnp.float32)[:, None, None] * frequency[None, None, :]
    first_half = key_rows[..., :half_width]
    second_half = key_rows[..., half_width:]
    cosine = jnp.cos(angles)
    sine_part = jnp.sin(angles)
    return jnp.concatenate([first_half * cosine - second_half * sine_part, second_half * cosine + first_half * sine_part], axis=-1)

def round_weights(weights):
    rounded = lax.optimization_barrier(weights.astype(jnp.bfloat16))
    return rounded.astype(jnp.float32)

def reference(hidden_state, norm_gain, kv_weight, queries, pool_keys, pool_values, page_table, lengths, move_target, move_page, move_request):
    group_size = QH // KVH
    scaling = 1.0 / math.sqrt(HD)
    widened = hidden_state.astype(jnp.float32)
    squares = lax.optimization_barrier(jnp.sum(widened * widened, axis=1)) / D
    inverse = lax.rsqrt(squares + EPSILON)
    normed = (widened * inverse[:, None] * norm_gain.astype(jnp.float32)[None, :]).astype(jnp.bfloat16)
    projected = jnp.dot(normed, kv_weight.reshape(D, KVH * 2 * HD), preferred_element_type=jnp.float32).reshape(ROWS, KVH, 2 * HD)
    rotated = rotate_keys(projected[:, :, :HD], lengths)
    new_kv = jnp.concatenate([rotated, projected[:, :, HD:]], axis=-1).astype(jnp.bfloat16)

    def local_part(inputs):
        query_inst, key_pool, value_pool, table_inst, length_inst, fresh_inst = inputs
        grouped = query_inst.astype(jnp.float32).reshape(REQ, KVH, group_size, HD)
        key_rows = key_pool[table_inst].astype(jnp.float32)
        value_rows = value_pool[table_inst].astype(jnp.float32)
        scores = jnp.einsum('rgqd,rigtd->rgqit', grouped, key_rows) * scaling
        token_pos = jnp.arange(MAXP, dtype=jnp.int32)[:, None] * PAGE + jnp.arange(PAGE, dtype=jnp.int32)[None, :]
        usable = (token_pos[None] < length_inst[:, None, None])[:, None, None]
        masked = jnp.where(usable, scores, FLOOR_SCORE)
        highest = lax.optimization_barrier(jnp.max(masked, axis=-1))
        weights = jnp.where(usable, jnp.exp(masked - highest[..., None]), 0.0)
        block_sum = lax.optimization_barrier(jnp.sum(weights, axis=-1))
        block_out = jnp.einsum('rgqit,rigtd->rgqid', round_weights(weights), value_rows)
        fresh_key = fresh_inst[:, :, :HD].astype(jnp.float32)
        fresh_value = fresh_inst[:, :, HD:].astype(jnp.float32)
        fresh_score = jnp.einsum('rgqd,rgd->rgq', grouped, fresh_key) * scaling
        row_best = jnp.maximum(lax.optimization_barrier(jnp.max(highest, axis=-1)), fresh_score)
        factor = jnp.exp(highest - row_best[..., None])
        fresh_factor = jnp.exp(fresh_score - row_best)
        denominator = lax.optimization_barrier(jnp.sum(factor * block_sum, axis=-1)) + fresh_factor
        numerator = lax.optimization_barrier(jnp.sum(factor[..., None] * block_out, axis=3)) + fresh_factor[..., None] * fresh_value[:, :, None, :]
        return (row_best, denominator, numerator)
    local_best, local_den, local_num = lax.map(local_part, (queries.reshape(N_INST, REQ, QH, HD), pool_keys.reshape(N_INST, POOL, KVH, PAGE, HD), pool_values.reshape(N_INST, POOL, KVH, PAGE, HD), page_table.reshape(N_INST, REQ, MAXP), lengths.reshape(N_INST, REQ), new_kv.reshape(N_INST, REQ, KVH, 2 * HD)))
    local_best = local_best.reshape(ROWS, KVH, group_size)
    local_den = local_den.reshape(ROWS, KVH, group_size)
    local_num = local_num.reshape(ROWS, KVH, group_size, HD)
    target_rows = (move_target[:, 0] * REQ + move_request).astype(jnp.int32)

    def moved_part(inputs):
        source, rows_here, pages_here = inputs
        grouped = queries[rows_here].astype(jnp.float32).reshape(MIG, KVH, group_size, HD)
        page_ids = (source * POOL + pages_here).astype(jnp.int32)
        key_page = pool_keys[page_ids].astype(jnp.float32)
        value_page = pool_values[page_ids].astype(jnp.float32)
        scores = jnp.einsum('mgqd,mgtd->mgqt', grouped, key_page) * scaling
        highest = lax.optimization_barrier(jnp.max(scores, axis=-1))
        weights = jnp.exp(scores - highest[..., None])
        block_sum = lax.optimization_barrier(jnp.sum(weights, axis=-1))
        block_out = jnp.einsum('mgqt,mgtd->mgqd', round_weights(weights), value_page)
        return (highest, block_sum, block_out)
    moved_high, moved_sum, moved_out = lax.map(moved_part, (jnp.arange(N_INST, dtype=jnp.int32), target_rows.reshape(N_INST, MIG), move_page.reshape(N_INST, MIG)))
    moved_high = moved_high.reshape(MIGS, KVH, group_size)
    moved_sum = moved_sum.reshape(MIGS, KVH, group_size)
    moved_out = moved_out.reshape(MIGS, KVH, group_size, HD)
    row_best = local_best.at[target_rows].max(moved_high)
    local_factor = jnp.exp(local_best - row_best)
    moved_factor = jnp.exp(moved_high - row_best[target_rows])
    denominator = local_den * local_factor + jnp.zeros_like(local_den).at[target_rows].add(moved_sum * moved_factor)
    numerator = local_num * local_factor[..., None] + jnp.zeros_like(local_num).at[target_rows].add(moved_out * moved_factor[..., None])
    attention_out = (numerator / denominator[..., None]).astype(jnp.bfloat16).reshape(ROWS, QH * HD)
    return (attention_out, new_kv)
```

```python
import functools
import math

import jax
import jax.numpy as jnp
from jax import lax
from jax.experimental import pallas as pl
from jax.experimental.pallas import tpu as pltpu
from jax.sharding import PartitionSpec as P

EPSILON = 1e-05
ROPE_BASE = 1000000.0
FLOOR = -1e30
WAIT = 6 * 10**9
LANES = 128
SLOTS = 8
LOG2E = 1.4426950408889634
VMEM = pl.BlockSpec(memory_space=pltpu.VMEM)
SMEM = pl.BlockSpec(memory_space=pltpu.SMEM)
ANY = pl.BlockSpec(memory_space=pl.ANY)
HBM = pl.BlockSpec(memory_space=pltpu.HBM)
F32 = jnp.float32
BF16 = jnp.bfloat16
NT = (((1,), (1,)), ((), ()))


def split_three(x):
    first = x.astype(BF16).astype(F32)
    second = (x - first).astype(BF16).astype(F32)
    third = (x - first - second).astype(BF16).astype(F32)
    return first, second, third


def slot_of(code, bits, root, slots):
    return lax.rem((code >> sum(bits)) + (slots - root), slots)


def label_kernel(bits, root, plan_ref, label_ref):
    label_ref[...] = jnp.full(label_ref.shape, -1, jnp.int32)
    for m in range(plan_ref.shape[0]):
        code = plan_ref[m]
        slot = slot_of(code, bits, root, label_ref.shape[0])
        request = (code >> bits[1]) & ((1 << bits[0]) - 1)
        label_ref[slot] = jnp.full((1, LANES), request, jnp.int32)


def ask_kernel(label_ref, query_ref, *rest):
    asked_ref = rest[-1]
    heads, requests, width = query_ref.shape
    slots = asked_ref.shape[0]
    labels = label_ref[...].reshape(slots, LANES)
    chosen = labels == lax.broadcasted_iota(jnp.int32, (slots, requests), 1)
    chosen = jnp.where(chosen, 1.0, 0.0).astype(BF16)
    rows = [jnp.dot(chosen, query_ref[h], preferred_element_type=F32) for h in range(heads)]
    rows += [jnp.zeros((slots, width), F32)] * (SLOTS - heads)
    asked_ref[...] = jnp.swapaxes(jnp.stack(rows), 0, 1).astype(BF16)


def moved_kernel(scale, heads, bits, root, plan_ref, asked_ref, key_ref, value_ref, *rest):
    out_ref, score_ref = rest[-2:]
    moves = plan_ref.shape[0]
    slots = [slot_of(plan_ref[m], bits, root, out_ref.shape[0]) for m in range(moves)]
    pages = [plan_ref[m] & ((1 << bits[1]) - 1) for m in range(moves)]
    for m in range(moves):
        score_ref[m] = lax.dot_general(
            asked_ref[slots[m]], key_ref[pages[m]], NT, preferred_element_type=F32
        )
    scores = score_ref[...] * scale
    highest = jnp.max(scores, axis=-1, keepdims=True)
    weights = jnp.exp2(scores - highest)
    sums = jnp.sum(weights, axis=-1, keepdims=True)
    level = jnp.broadcast_to(highest + jnp.log(sums) * LOG2E, scores.shape)
    row = lax.broadcasted_iota(jnp.int32, scores.shape, 1)
    lane = lax.broadcasted_iota(jnp.int32, scores.shape, 2)
    level = jnp.sum(
        jnp.where((lane % SLOTS == row) & (row < heads), level, 0.0), axis=1, keepdims=True
    )
    first, second, third = split_three(jnp.broadcast_to(level, scores.shape))
    part = lane // SLOTS
    stats = jnp.where(part == 0, first, jnp.where(part == 1, second, third))
    inverse = 1.0 / sums
    rounded = weights.astype(BF16)
    out_ref[...] = jnp.zeros(out_ref.shape, out_ref.dtype)
    for m in range(moves):
        product = jnp.dot(rounded[m], value_ref[pages[m]], preferred_element_type=F32)
        product = product * inverse[m]
        message = jnp.where(row[m] < heads, product, stats[m])
        out_ref[slots[m]] = message.astype(BF16)


def local_kernel(scale, first, query_ref, key_ref, value_ref, table_ref, length_ref, out_ref, stat_ref, bias_ref, score_ref):
    heads, requests, width = out_ref.shape
    pool, page_len, _ = key_ref.shape
    pairs = pool // 2
    entries = table_ref.shape[0]
    lengths = length_ref[...]
    page = lax.broadcasted_iota(jnp.int32, (LANES, requests), 0)
    counts = jnp.zeros((LANES, requests), jnp.int32)
    for i in range(entries):
        held = jnp.clip(lengths - i * page_len, 0, page_len)
        counts = counts + jnp.where(table_ref[i : i + 1, :] == page, held, 0)
    counts = counts.astype(F32).T
    token = lax.broadcasted_iota(jnp.int32, (requests, page_len), 1).astype(F32)
    for p in range(pool):
        bias_ref[p // 2, :, (p % 2) * page_len : (p % 2 + 1) * page_len] = jnp.where(
            token < counts[:, p : p + 1], 0.0, FLOOR
        )
    query = query_ref[first : first + heads].reshape(heads * requests, width)
    best = jnp.full((heads, requests, 2 * page_len), FLOOR, F32)
    for p in range(pairs):
        keys = key_ref[2 * p : 2 * p + 2].reshape(2 * page_len, width)
        scores = lax.dot_general(query, keys, NT, preferred_element_type=F32)
        scores = scores.reshape(heads, requests, 2 * page_len) * scale + bias_ref[p][None]
        score_ref[p] = scores
        best = jnp.maximum(best, scores)
    best = jnp.max(best, axis=-1, keepdims=True)
    total = jnp.zeros((heads, requests, 2 * page_len), F32)
    out = jnp.zeros((heads * requests, width), F32)
    for p in range(pairs):
        values = value_ref[2 * p : 2 * p + 2].reshape(2 * page_len, width)
        weights = jnp.exp2(score_ref[p] - best)
        total = total + weights
        rounded = weights.astype(BF16).reshape(heads * requests, 2 * page_len)
        out = out + jnp.dot(rounded, values, preferred_element_type=F32)
    out_ref[...] = out.reshape(heads, requests, width)
    total = jnp.sum(total, axis=-1, keepdims=True)
    lane = lax.broadcasted_iota(jnp.int32, (requests, LANES), 1)
    stats = jnp.zeros((requests, LANES), F32)
    for h in range(heads):
        stats = jnp.where(lane == first + h, best[h], stats)
        stats = jnp.where(lane == SLOTS + first + h, total[h], stats)
    stat_ref[...] = stats


def norm_kernel(hidden_ref, gain_ref, _, scaled_ref, extra_ref):
    widened = hidden_ref[...].astype(F32)
    requests = widened.shape[0]
    scaled_ref[...] = (widened * gain_ref[...].astype(F32).reshape(1, -1)).astype(BF16)
    squares = jnp.sum(widened * widened, axis=1, keepdims=True)
    row = lax.broadcasted_iota(jnp.int32, (requests, LANES), 0)
    lane = lax.broadcasted_iota(jnp.int32, (requests, LANES), 1)
    squares = jnp.sum(jnp.where(row == lane, squares, 0.0), axis=0, keepdims=True)
    first, second, third = split_three(squares)
    upper = jnp.concatenate([first, second], axis=1)
    lower = jnp.concatenate([third, jnp.zeros_like(third)], axis=1)
    place = lax.broadcasted_iota(jnp.int32, extra_ref.shape, 0) - 2 * lax.axis_index("tp")
    extra_ref[...] = jnp.where(place == 0, upper, jnp.where(place == 1, lower, 0.0))


def bits():
    rank = lax.axis_index("tp")
    return rank // 2 % 2, rank // 4, rank % 2


def first_kernel(partial_ref, extra_ref, send_ref, keep_ref):
    near, _, _ = bits()
    rows = partial_ref.shape[1]
    for i in range(2):
        for j in range(2):
            keep_ref[i, j, :rows] = partial_ref[4 * i + 2 * near + j]
            keep_ref[i, j, rows:] = extra_ref[...]
            send_ref[i, j, :rows] = partial_ref[4 * i + 2 * (1 - near) + j].astype(BF16)
            send_ref[i, j, rows:] = extra_ref[...].astype(BF16)


def second_kernel(got_ref, kept_ref, _, send_ref, keep_ref):
    _, far, _ = bits()
    keep_ref[...] = kept_ref[far] + got_ref[far].astype(F32)
    send_ref[...] = (kept_ref[1 - far] + got_ref[1 - far].astype(F32)).astype(BF16)


def third_kernel(got_ref, keep_ref, _, send_ref, last_ref):
    mid = bits()[2]
    last_ref[...] = keep_ref[mid] + got_ref[mid].astype(F32)
    send_ref[...] = (keep_ref[1 - mid] + got_ref[1 - mid].astype(F32)).astype(BF16)


def fresh_kernel(scale, features, got_ref, last_ref, cos_ref, sin_ref, query_ref, out_a_ref, stat_a_ref, out_b_ref, stat_b_ref, kv_ref, new_out_ref, new_stat_ref):
    heads, requests, width = query_ref.shape
    part = out_a_ref.shape[0]
    total = last_ref[...] + got_ref[...].astype(F32)
    extra = jnp.sum(total[requests:], axis=0, keepdims=True)
    squares = extra[:, :LANES] + extra[:, LANES:]
    row = lax.broadcasted_iota(jnp.int32, (requests, LANES), 0)
    lane = lax.broadcasted_iota(jnp.int32, (requests, LANES), 1)
    squares = jnp.sum(jnp.where(row == lane, squares, 0.0), axis=1, keepdims=True)
    inverse = lax.rsqrt(squares / features + EPSILON)
    projected = total[:requests] * inverse
    key = projected[:, :width]
    key = key * cos_ref[...] + pltpu.roll(key, width // 2, 1) * sin_ref[...]
    key = key.astype(BF16)
    value = projected[:, width:].astype(BF16)
    kv_ref[:, :width] = key
    kv_ref[:, width:] = value
    key = key.astype(F32)
    value = value.astype(F32)
    stats = stat_a_ref[...] + stat_b_ref[...]
    new_stats = jnp.zeros((requests, LANES), F32)
    for h in range(heads):
        score = jnp.sum(query_ref[h].astype(F32) * key, axis=1, keepdims=True) * scale
        highest = stats[:, h : h + 1]
        best = jnp.maximum(highest, score)
        factor = jnp.exp2(highest - best)
        fresh = jnp.exp2(score - best)
        out = out_a_ref[h] if h < part else out_b_ref[h - part]
        new_out_ref[h] = out * factor + fresh * value
        sums = stats[:, SLOTS + h : SLOTS + h + 1] * factor + fresh
        new_stats = jnp.where(lane == h, best, new_stats)
        new_stats = jnp.where(lane == SLOTS + h, sums, new_stats)
    new_stat_ref[...] = new_stats


def owner_kernel(label_ref, owner_ref):
    requests, slots = owner_ref.shape
    labels = label_ref[...].reshape(slots, LANES).T
    owner_ref[...] = jnp.where(
        labels == lax.broadcasted_iota(jnp.int32, (requests, slots), 0), 0.0, FLOOR
    )


def combine_kernel(message_ref, owner_ref, out_ref, stat_ref, final_ref):
    heads, requests, width = out_ref.shape
    messages = jnp.swapaxes(message_ref[...].astype(F32), 0, 1)
    levels = messages[heads].T
    levels = levels[0:SLOTS] + levels[SLOTS : 2 * SLOTS] + levels[2 * SLOTS : 3 * SLOTS]
    bias = owner_ref[...]
    stats = stat_ref[...]
    for h in range(heads):
        scores = bias + levels[h : h + 1]
        highest = stats[:, h : h + 1]
        best = jnp.maximum(highest, jnp.max(scores, axis=1, keepdims=True))
        weights = jnp.exp2(scores - best)
        factor = jnp.exp2(highest - best)
        sums = stats[:, SLOTS + h : SLOTS + h + 1] * factor + jnp.sum(weights, axis=1, keepdims=True)
        coarse = weights.astype(BF16)
        fine = (weights - coarse.astype(F32)).astype(BF16)
        moved = messages[h].astype(BF16)
        total = (
            out_ref[h] * factor
            + jnp.dot(coarse, moved, preferred_element_type=F32)
            + jnp.dot(fine, moved, preferred_element_type=F32)
        )
        final_ref[:, h * width : (h + 1) * width] = (total / sums).astype(BF16)


def call(kernel, shapes, ins, scratch=(), limit=8, flops=10**9, moved=0):
    return pl.pallas_call(
        kernel,
        out_shape=shapes,
        in_specs=ins,
        out_specs=jax.tree.map(lambda _: VMEM, shapes),
        scratch_shapes=scratch,
        compiler_params=pltpu.CompilerParams(vmem_limit_bytes=limit * 1024 * 1024),
        cost_estimate=pl.CostEstimate(flops=flops, bytes_accessed=moved, transcendentals=0),
    )


def rotation(lengths, width):
    steps = jnp.arange(width // 2, dtype=F32)
    frequency = ROPE_BASE ** (-2.0 * steps / width)
    angles = lengths.astype(F32)[:, None] * frequency[None, :]
    cosine = jnp.cos(angles)
    sine = jnp.sin(angles)
    return jnp.concatenate([cosine, cosine], axis=1), jnp.concatenate([-sine, sine], axis=1)


def body(
    hidden_state,
    norm_gain,
    kv_weight,
    queries,
    pool_keys,
    pool_values,
    page_table,
    lengths,
    move_target,
    move_page,
    move_request,
):
    shape = jax.ShapeDtypeStruct
    requests, heads, width = queries.shape
    pool, _, page_len, _ = pool_keys.shape
    moves = move_page.shape[0]
    instances = lax.axis_size("inst")
    ranks = lax.axis_size("tp")
    features = hidden_state.shape[1] * ranks
    scale = LOG2E / math.sqrt(width)
    root = instances * 25 // 32
    order = [(i + root) % instances for i in range(instances)]

    def exchange(x):
        return lax.all_to_all(x, "inst", 0, 0, tiled=True, axis_index_groups=[order])


    def swap(x, bit):
        return lax.ppermute(x, "tp", [(i, i ^ bit) for i in range(ranks)])

    keys = pool_keys.reshape(pool, page_len, width)
    values = pool_values.reshape(pool, page_len, width)
    by_head = jnp.transpose(queries, (1, 0, 2))

    bits = ((requests - 1).bit_length(), (pool - 1).bit_length())
    plan = (((move_target[:, 0] << bits[0]) | move_request) << bits[1]) | move_page
    labels = call(
        functools.partial(label_kernel, bits, root),
        shape((instances, 1, LANES), jnp.int32),
        [SMEM],
        flops=10**10,
    )(plan)
    labels = exchange(labels)

    scaled, extra = call(
        norm_kernel,
        [shape(hidden_state.shape, BF16), shape((16, 2 * width), F32)],
        [VMEM, VMEM, ANY],
    )(hidden_state, norm_gain, kv_weight)
    partial = jnp.einsum("rf,fgc->grc", scaled, kv_weight, preferred_element_type=F32)
    padded = requests + 16
    send, keep = call(
        first_kernel,
        [shape((2, 2, padded, 2 * width), BF16), shape((2, 2, padded, 2 * width), F32)],
        [VMEM, VMEM],
    )(partial, extra)
    got = swap(send, 2)

    def local(first, count, weight):
        return call(
            functools.partial(local_kernel, scale, first),
            [shape((count, requests, width), F32), shape((requests, LANES), F32)],
            [VMEM] * 5,
            [
                pltpu.VMEM((pool // 2, requests, 2 * page_len), F32),
                pltpu.VMEM((pool // 2, count, requests, 2 * page_len), F32),
            ],
            limit=16,
            flops=4 * weight * count * requests * pool * page_len * width,
            moved=4 * pool * page_len * width,
        )(by_head, keys, values, page_table.T, lengths[None, :])

    asked = call(ask_kernel, shape((instances, SLOTS, width), BF16), [VMEM, VMEM, ANY])(labels, by_head, send)
    asked = exchange(asked)

    out_a, stat_a = local(0, heads // 2, 12)
    send, keep = call(
        second_kernel,
        [shape((2, padded, 2 * width), BF16), shape((2, padded, 2 * width), F32)],
        [VMEM, VMEM, ANY],
    )(got, keep, stat_a)
    got = swap(send, 4)

    answers = call(
        functools.partial(moved_kernel, scale, heads, bits, root),
        shape((instances, SLOTS, width), BF16),
        [SMEM, VMEM, VMEM, VMEM, ANY],
        [pltpu.VMEM((moves, SLOTS, page_len), F32)],
    )(plan, asked, keys, values, send)
    answers = exchange(answers)

    owner = call(
        owner_kernel, shape((requests, instances), F32), [VMEM], flops=WAIT
    )(labels)
    out_b, stat_b = local(heads // 2, heads - heads // 2, 1)
    send, last = call(
        third_kernel,
        [shape((padded, 2 * width), BF16), shape((padded, 2 * width), F32)],
        [VMEM, VMEM, ANY],
    )(got, keep, owner)
    got = swap(send, 1)
    cosine, sine = rotation(lengths, width)
    new_kv, out, stats = call(
        functools.partial(fresh_kernel, scale, features),
        [
            shape((requests, 2 * width), BF16),
            shape((heads, requests, width), F32),
            shape((requests, LANES), F32),
        ],
        [VMEM] * 9,
    )(got, last, cosine, sine, by_head, out_a, stat_a, out_b, stat_b)
    attention_out = call(combine_kernel, shape((requests, heads * width), BF16), [VMEM] * 4)(
        answers, owner, out, stats
    )
    return (attention_out, new_kv.reshape(requests, 1, 2 * width))


def solution(mesh):
    return jax.shard_map(
        body,
        mesh=mesh,
        in_specs=(
            P("inst", "tp"),
            P("tp"),
            P("tp", None, None),
            P("inst", "tp", None),
            P("inst", "tp", None, None),
            P("inst", "tp", None, None),
            P("inst", None),
            P("inst"),
            P("inst", None),
            P("inst"),
            P("inst"),
        ),
        out_specs=(P("inst", "tp"), P("inst", "tp", None)),
        check_vma=False,
    )
```

```python
import functools
import math

import jax
import jax.numpy as jnp
from jax import lax
from jax.experimental import pallas as pl
from jax.experimental.pallas import tpu as pltpu
from jax.sharding import PartitionSpec as P

EPSILON = 1e-05
ROPE_BASE = 1000000.0
FLOOR = -1e30
SECOND = 0
THIRD = 10**9
LATER = 2 * 10**8
LANES = 128
SLOTS = 8
LOG2E = 1.4426950408889634
VMEM = pl.BlockSpec(memory_space=pltpu.VMEM)
SMEM = pl.BlockSpec(memory_space=pltpu.SMEM)
ANY = pl.BlockSpec(memory_space=pl.ANY)
HBM = pl.BlockSpec(memory_space=pltpu.HBM)
F32 = jnp.float32
BF16 = jnp.bfloat16
NT = (((1,), (1,)), ((), ()))
TN = (((0,), (0,)), ((), ()))


def split_three(x):
    first = x.astype(BF16).astype(F32)
    second = (x - first).astype(BF16).astype(F32)
    third = (x - first - second).astype(BF16).astype(F32)
    return first, second, third


def slot_of(code, bits, root, slots):
    return lax.rem((code >> sum(bits)) + (slots - root), slots)


def label_kernel(bits, root, plan_ref, label_ref):
    slots = label_ref.shape[0]
    plan = plan_ref[...]
    place = slot_of(plan, bits, root, slots)
    request = (plan >> bits[1]) & ((1 << bits[0]) - 1)
    named = place == lax.broadcasted_iota(jnp.int32, (slots, plan.shape[1]), 0)
    found = jnp.sum(jnp.where(named, request + 1, 0), axis=1, keepdims=True) - 1
    label_ref[...] = jnp.broadcast_to(found, (slots, LANES)).reshape(slots, 1, LANES)


def ask_kernel(label_ref, query_ref, *rest):
    asked_ref = rest[-1]
    heads, requests, width = query_ref.shape
    slots = asked_ref.shape[0]
    labels = label_ref[...].reshape(slots, LANES)
    chosen = labels == lax.broadcasted_iota(jnp.int32, (slots, requests), 1)
    chosen = jnp.where(chosen, 1.0, 0.0).astype(BF16)
    rows = [jnp.dot(chosen, query_ref[h], preferred_element_type=F32) for h in range(heads)]
    halves = [jnp.concatenate(rows[i::2], axis=1) for i in range(2)]
    asked_ref[...] = jnp.swapaxes(jnp.stack(halves), 0, 1).astype(BF16)


def moved_kernel(scale, heads, bits, root, plan_ref, asked_ref, key_ref, value_ref, *rest):
    out_ref, score_ref = rest[-2:]
    moves = plan_ref.shape[1]
    width = out_ref.shape[2]
    plan = [plan_ref[0, m] for m in range(moves)]
    slots = [slot_of(code, bits, root, out_ref.shape[0]) for code in plan]
    pages = [code & ((1 << bits[1]) - 1) for code in plan]
    spare = jnp.zeros((SLOTS - heads, width), F32)
    for m in range(moves):
        pairs = asked_ref[slots[m]].astype(F32)
        query = [pairs[:, i * width : (i + 1) * width] for i in range(heads // 2)]
        query = jnp.concatenate(query + [spare], axis=0).astype(BF16)
        score_ref[m] = lax.dot_general(
            query, key_ref[pages[m]], NT, preferred_element_type=F32
        )
    scores = score_ref[...] * scale
    highest = jnp.max(scores, axis=-1, keepdims=True)
    weights = jnp.exp2(scores - highest)
    sums = jnp.sum(weights, axis=-1, keepdims=True)
    level = jnp.broadcast_to(highest + jnp.log(sums) * LOG2E, scores.shape)
    row = lax.broadcasted_iota(jnp.int32, scores.shape, 1)
    lane = lax.broadcasted_iota(jnp.int32, scores.shape, 2)
    level = jnp.sum(
        jnp.where((lane % SLOTS == row) & (row < heads), level, 0.0), axis=1, keepdims=True
    )
    first, second, third = split_three(jnp.broadcast_to(level, scores.shape))
    part = lane // SLOTS
    stats = jnp.where(part == 0, first, jnp.where(part == 1, second, third))
    inverse = 1.0 / sums
    rounded = weights.astype(BF16)
    out_ref[...] = jnp.zeros(out_ref.shape, out_ref.dtype)
    for m in range(moves):
        product = jnp.dot(rounded[m], value_ref[pages[m]], preferred_element_type=F32)
        product = product * inverse[m]
        message = jnp.where(row[m] < heads, product, stats[m])
        out_ref[slots[m]] = message.astype(BF16)


def local_kernel(scale, first, query_ref, key_ref, value_ref, table_ref, length_ref, *rest):
    out_ref, stat_ref, bias_ref, score_ref = rest[-4:]
    heads, requests, width = out_ref.shape
    heads = heads - first
    pool, page_len, _ = key_ref.shape
    pairs = pool // 2
    entries = table_ref.shape[0]
    lengths = length_ref[...]
    page = lax.broadcasted_iota(jnp.int32, (LANES, requests), 0)
    counts = jnp.zeros((LANES, requests), jnp.int32)
    for i in range(entries):
        held = jnp.clip(lengths - i * page_len, 0, page_len)
        counts = counts + jnp.where(table_ref[i : i + 1, :] == page, held, 0)
    counts = counts.astype(F32).T
    token = lax.broadcasted_iota(jnp.int32, (requests, page_len), 1).astype(F32)
    for p in range(pool):
        bias_ref[p // 2, :, (p % 2) * page_len : (p % 2 + 1) * page_len] = jnp.where(
            token < counts[:, p : p + 1], 0.0, FLOOR
        )
    query = query_ref[first : first + heads].reshape(heads * requests, width)
    best = jnp.full((heads, requests, 2 * page_len), FLOOR, F32)
    for p in range(pairs):
        keys = key_ref[2 * p : 2 * p + 2].reshape(2 * page_len, width)
        scores = lax.dot_general(query, keys, NT, preferred_element_type=F32)
        scores = scores.reshape(heads, requests, 2 * page_len) * scale + bias_ref[p][None]
        score_ref[p] = scores
        best = jnp.maximum(best, scores)
    best = jnp.max(best, axis=-1, keepdims=True)
    total = jnp.zeros((heads, requests, 2 * page_len), F32)
    out = jnp.zeros((heads * requests, width), F32)
    for p in range(pairs):
        values = value_ref[2 * p : 2 * p + 2].reshape(2 * page_len, width)
        weights = jnp.exp2(score_ref[p] - best)
        total = total + weights
        rounded = weights.astype(BF16).reshape(heads * requests, 2 * page_len)
        out = out + jnp.dot(rounded, values, preferred_element_type=F32)
    out_ref[first:] = out.reshape(heads, requests, width)
    total = jnp.sum(total, axis=-1, keepdims=True)
    lane = lax.broadcasted_iota(jnp.int32, (requests, LANES), 1)
    stats = jnp.zeros((requests, LANES), F32)
    for h in range(heads):
        stats = jnp.where(lane == first + h, best[h], stats)
        stats = jnp.where(lane == SLOTS + first + h, total[h], stats)
    stats = stats.T[: 2 * SLOTS]
    if first:
        out_ref[:first] = rest[0][...]
        stats = stats + rest[1][...]
    stat_ref[...] = stats


def norm_kernel(hidden_ref, gain_ref, _, scaled_ref, extra_ref):
    widened = hidden_ref[...].astype(F32)
    requests = widened.shape[0]
    scaled_ref[...] = (widened * gain_ref[...].astype(F32).reshape(1, -1)).astype(BF16)
    squares = jnp.sum(widened * widened, axis=1, keepdims=True)
    row = lax.broadcasted_iota(jnp.int32, (requests, LANES), 0)
    lane = lax.broadcasted_iota(jnp.int32, (requests, LANES), 1)
    squares = jnp.sum(jnp.where(row == lane, squares, 0.0), axis=0, keepdims=True)
    first, second, third = split_three(squares)
    upper = jnp.concatenate([first, second], axis=1)
    lower = jnp.concatenate([third, jnp.zeros_like(third)], axis=1)
    place = lax.broadcasted_iota(jnp.int32, extra_ref.shape, 0) - 2 * lax.axis_index("tp")
    extra_ref[...] = jnp.where(place == 0, upper, jnp.where(place == 1, lower, 0.0))


def place():
    rank = lax.axis_index("tp")
    return rank // 4, rank % 2, rank // 2 % 2


def first_kernel(partial_ref, extra_ref, send_ref, keep_ref):
    _, side, _ = place()
    rows = partial_ref.shape[1]
    for i in range(2):
        for j in range(2):
            keep_ref[i, j, :rows] = partial_ref[4 * i + 2 * j + side]
            keep_ref[i, j, rows:] = extra_ref[...]
            send_ref[i, j, :rows] = partial_ref[4 * i + 2 * j + 1 - side].astype(BF16)
            send_ref[i, j, rows:] = extra_ref[...].astype(BF16)


def second_kernel(got_ref, kept_ref, _, send_ref, keep_ref):
    far, _, _ = place()
    keep_ref[...] = kept_ref[far] + got_ref[far].astype(F32)
    send_ref[...] = (kept_ref[1 - far] + got_ref[1 - far].astype(F32)).astype(BF16)


def third_kernel(got_ref, kept_ref, length_ref, frequency_ref, send_ref, last_ref, angle_ref):
    _, _, near = place()
    last_ref[...] = kept_ref[near] + got_ref[near].astype(F32)
    send_ref[...] = (kept_ref[1 - near] + got_ref[1 - near].astype(F32)).astype(BF16)
    requests, half = angle_ref.shape
    lengths = jnp.broadcast_to(length_ref[...].astype(F32), (LANES, requests)).T
    angle_ref[...] = lengths[:, :half] * frequency_ref[...]


def fresh_kernel(scale, features, got_ref, last_ref, cos_ref, sin_ref, query_ref, kv_ref, value_ref, score_ref):
    heads, requests, width = query_ref.shape
    total = last_ref[...] + got_ref[...].astype(F32)
    extra = jnp.sum(total[requests:], axis=0, keepdims=True)
    squares = extra[:, :LANES] + extra[:, LANES:]
    row = lax.broadcasted_iota(jnp.int32, (requests, LANES), 0)
    lane = lax.broadcasted_iota(jnp.int32, (requests, LANES), 1)
    squares = jnp.sum(jnp.where(row == lane, squares, 0.0), axis=1, keepdims=True)
    inverse = lax.rsqrt(squares / features + EPSILON)
    projected = total[:requests] * inverse
    key = projected[:, :width]
    key = key * cos_ref[...] + pltpu.roll(key, width // 2, 1) * sin_ref[...]
    key = key.astype(BF16)
    kv_ref[:, :width] = key
    value = projected[:, width:].astype(BF16)
    kv_ref[:, width:] = value
    value_ref[...] = value.astype(F32)
    key = key.astype(F32)
    scores = jnp.zeros((requests, LANES), F32)
    for h in range(heads):
        score = jnp.sum(query_ref[h].astype(F32) * key, axis=1, keepdims=True)
        scores = jnp.where(lane == h, score * scale, scores)
    score_ref[...] = scores.T[:SLOTS]


def owner_kernel(label_ref, owner_ref):
    slots, requests = owner_ref.shape
    labels = label_ref[...].reshape(slots, LANES)
    owner_ref[...] = jnp.where(
        labels == lax.broadcasted_iota(jnp.int32, (slots, requests), 1), 0.0, FLOOR
    )


def combine_kernel(message_ref, owner_ref, out_ref, stat_ref, fresh_ref, value_ref, final_ref):
    heads, requests, width = out_ref.shape
    messages = jnp.swapaxes(message_ref[...].astype(F32), 0, 1)
    levels = messages[heads]
    levels = levels[:, :SLOTS] + levels[:, SLOTS : 2 * SLOTS] + levels[:, 2 * SLOTS : 3 * SLOTS]
    owner = owner_ref[...]
    scores = [owner + levels[:, h : h + 1] for h in range(heads)]
    rows = [jnp.max(score, axis=0, keepdims=True) for score in scores]
    moved_best = jnp.concatenate(rows + [rows[0]] * (SLOTS - heads), axis=0)
    stats = stat_ref[...]
    highest = stats[:SLOTS]
    fresh = fresh_ref[...]
    best = jnp.maximum(jnp.maximum(highest, fresh), moved_best)
    weights = [jnp.exp2(scores[h] - best[h : h + 1]) for h in range(heads)]
    rows = [jnp.sum(weight, axis=0, keepdims=True) for weight in weights]
    moved_sums = jnp.concatenate(rows + [rows[0]] * (SLOTS - heads), axis=0)
    factor = jnp.exp2(highest - best)
    fresh = jnp.exp2(fresh - best)
    inverse = 1.0 / (stats[SLOTS:] * factor + fresh + moved_sums)
    columns = jnp.concatenate(
        [factor * inverse, fresh * inverse, jnp.zeros((LANES - 2 * SLOTS, requests), F32)], axis=0
    ).T
    value = value_ref[...]
    for h in range(heads):
        weight = weights[h] * inverse[h : h + 1]
        coarse = weight.astype(BF16)
        fine = (weight - coarse.astype(F32)).astype(BF16)
        moved = messages[h].astype(BF16)
        total = lax.dot_general(
            jnp.concatenate([coarse, fine], axis=0),
            jnp.concatenate([moved, moved], axis=0),
            TN,
            preferred_element_type=F32,
        )
        total = total + out_ref[h] * columns[:, h : h + 1] + value * columns[:, SLOTS + h : SLOTS + h + 1]
        final_ref[:, h * width : (h + 1) * width] = total.astype(BF16)


def call(kernel, shapes, ins, scratch=(), limit=8, flops=10**9, moved=0):
    return pl.pallas_call(
        kernel,
        out_shape=shapes,
        in_specs=ins,
        out_specs=jax.tree.map(lambda _: VMEM, shapes),
        scratch_shapes=scratch,
        compiler_params=pltpu.CompilerParams(vmem_limit_bytes=limit * 1024 * 1024),
        cost_estimate=pl.CostEstimate(flops=flops, bytes_accessed=moved, transcendentals=0),
    )


def frequencies(width):
    steps = jnp.arange(width // 2, dtype=F32)
    return (ROPE_BASE ** (-2.0 * steps / width))[None, :]


def body(
    hidden_state,
    norm_gain,
    kv_weight,
    queries,
    pool_keys,
    pool_values,
    page_table,
    lengths,
    move_target,
    move_page,
    move_request,
):
    shape = jax.ShapeDtypeStruct
    requests, heads, width = queries.shape
    pool, _, page_len, _ = pool_keys.shape
    moves = move_page.shape[0]
    instances = lax.axis_size("inst")
    ranks = lax.axis_size("tp")
    features = hidden_state.shape[1] * ranks
    scale = LOG2E / math.sqrt(width)
    root = instances * 25 // 32
    order = [(i + root) % instances for i in range(instances)]

    def exchange(x):
        return lax.all_to_all(x, "inst", 0, 0, tiled=True, axis_index_groups=[order])


    def swap(x, bit):
        return lax.ppermute(x, "tp", [(i, i ^ bit) for i in range(ranks)])

    keys = pool_keys.reshape(pool, page_len, width)
    values = pool_values.reshape(pool, page_len, width)
    by_head = jnp.transpose(queries, (1, 0, 2))

    bits = ((requests - 1).bit_length(), (pool - 1).bit_length())
    plan = (((move_target[:, 0] << bits[0]) | move_request) << bits[1]) | move_page
    labels = call(
        functools.partial(label_kernel, bits, root),
        shape((instances, 1, LANES), jnp.int32),
        [VMEM],
        flops=10**10,
    )(plan.reshape(1, moves))
    labels = exchange(labels)

    scaled, extra = call(
        norm_kernel,
        [shape(hidden_state.shape, BF16), shape((16, 2 * width), F32)],
        [VMEM, VMEM, ANY],
    )(hidden_state, norm_gain, kv_weight)
    partial = jnp.einsum("rf,fgc->grc", scaled, kv_weight, preferred_element_type=F32)
    padded = requests + 16
    send, keep = call(
        first_kernel,
        [shape((2, 2, padded, 2 * width), BF16), shape((2, 2, padded, 2 * width), F32)],
        [VMEM, VMEM],
    )(partial, extra)
    got = swap(send, 1)

    def local(first, stop, cost, *earlier):
        return call(
            functools.partial(local_kernel, scale, first),
            [shape((stop, requests, width), F32), shape((2 * SLOTS, requests), F32)],
            [VMEM] * 5 + [VMEM, VMEM, ANY][: len(earlier)],
            [
                pltpu.VMEM((pool // 2, requests, 2 * page_len), F32),
                pltpu.VMEM((pool // 2, stop - first, requests, 2 * page_len), F32),
            ],
            limit=16,
            flops=cost,
        )(by_head, keys, values, page_table.T, lengths[None, :], *earlier)

    asked = call(ask_kernel, shape((instances, 2, heads // 2 * width), BF16), [VMEM, VMEM, ANY])(labels, by_head, send)
    asked = exchange(asked)

    out, stats = local(0, heads // 2, 3 * 10**9)
    send, keep = call(
        second_kernel,
        [shape((2, padded, 2 * width), BF16), shape((2, padded, 2 * width), F32)],
        [VMEM, VMEM, ANY],
        flops=SECOND,
    )(got, keep, stats)
    got = swap(send, 4)

    answers = call(
        functools.partial(moved_kernel, scale, heads, bits, root),
        shape((instances, SLOTS, width), BF16),
        [VMEM, VMEM, VMEM, VMEM, ANY],
        [pltpu.VMEM((moves, SLOTS, page_len), F32)],
    )(plan.reshape(1, moves), asked, keys, values, send)
    answers = exchange(answers)

    owner = call(
        owner_kernel, shape((instances, requests), F32), [VMEM], flops=0
    )(labels)
    send, last, angles = call(
        third_kernel,
        [
            shape((padded, 2 * width), BF16),
            shape((padded, 2 * width), F32),
            shape((requests, width // 2), F32),
        ],
        [VMEM] * 4,
        flops=THIRD,
    )(got, keep, lengths[None, :], frequencies(width))
    out, stats = local(heads // 2, heads, LATER, out, stats, send)
    got = swap(send, 2)
    cosine = jnp.cos(angles)
    sine = jnp.sin(angles)
    cosine = jnp.concatenate([cosine, cosine], axis=1)
    sine = jnp.concatenate([-sine, sine], axis=1)
    new_kv, value, fresh = call(
        functools.partial(fresh_kernel, scale, features),
        [shape((requests, 2 * width), BF16), shape((requests, width), F32), shape((SLOTS, requests), F32)],
        [VMEM] * 5,
    )(got, last, cosine, sine, by_head)
    attention_out = call(combine_kernel, shape((requests, heads * width), BF16), [VMEM] * 6)(
        answers, owner, out, stats, fresh, value
    )
    return (attention_out, new_kv.reshape(requests, 1, 2 * width))


def solution(mesh):
    return jax.shard_map(
        body,
        mesh=mesh,
        in_specs=(
            P("inst", "tp"),
            P("tp"),
            P("tp", None, None),
            P("inst", "tp", None),
            P("inst", "tp", None, None),
            P("inst", "tp", None, None),
            P("inst", None),
            P("inst"),
            P("inst", None),
            P("inst"),
            P("inst"),
        ),
        out_specs=(P("inst", "tp"), P("inst", "tp", None)),
        check_vma=False,
    )
```

```python
import functools
import math

import jax
import jax.numpy as jnp
from jax import lax
from jax.experimental import pallas as pl
from jax.experimental.pallas import tpu as pltpu
from jax.sharding import PartitionSpec as P

EPSILON = 1e-05
ROPE_BASE = 1000000.0
FLOOR = -1e30
SECOND = 0
THIRD = 10**9
LATER = 2 * 10**8
LANES = 128
SLOTS = 8
LOG2E = 1.4426950408889634
VMEM = pl.BlockSpec(memory_space=pltpu.VMEM)
SMEM = pl.BlockSpec(memory_space=pltpu.SMEM)
ANY = pl.BlockSpec(memory_space=pl.ANY)
HBM = pl.BlockSpec(memory_space=pltpu.HBM)
F32 = jnp.float32
BF16 = jnp.bfloat16
NT = (((1,), (1,)), ((), ()))
TN = (((0,), (0,)), ((), ()))


def split_three(x):
    first = x.astype(BF16).astype(F32)
    second = (x - first).astype(BF16).astype(F32)
    third = (x - first - second).astype(BF16).astype(F32)
    return first, second, third


def slot_of(code, bits, root, slots):
    return lax.rem((code >> sum(bits)) + (slots - root), slots)


def label_kernel(bits, root, plan_ref, label_ref):
    slots = label_ref.shape[0]
    plan = plan_ref[...]
    place = slot_of(plan, bits, root, slots)
    request = (plan >> bits[1]) & ((1 << bits[0]) - 1)
    named = place == lax.broadcasted_iota(jnp.int32, (slots, plan.shape[1]), 0)
    found = jnp.sum(jnp.where(named, request + 1, 0), axis=1, keepdims=True) - 1
    label_ref[...] = jnp.broadcast_to(found, (slots, LANES)).reshape(slots, 1, LANES)


def ask_kernel(label_ref, query_ref, *rest):
    asked_ref = rest[-1]
    heads, requests, width = query_ref.shape
    slots = asked_ref.shape[0]
    labels = label_ref[...].reshape(slots, LANES)
    chosen = labels == lax.broadcasted_iota(jnp.int32, (slots, requests), 1)
    chosen = jnp.where(chosen, 1.0, 0.0).astype(BF16)
    rows = [jnp.dot(chosen, query_ref[h], preferred_element_type=F32) for h in range(heads)]
    halves = [jnp.concatenate(rows[i::2], axis=1) for i in range(2)]
    asked_ref[...] = jnp.swapaxes(jnp.stack(halves), 0, 1).astype(BF16)


def moved_kernel(scale, heads, bits, root, plan_ref, asked_ref, key_ref, value_ref, *rest):
    out_ref, score_ref = rest[-2:]
    moves = plan_ref.shape[1]
    width = out_ref.shape[2]
    plan = [plan_ref[0, m] for m in range(moves)]
    slots = [slot_of(code, bits, root, out_ref.shape[0]) for code in plan]
    pages = [code & ((1 << bits[1]) - 1) for code in plan]
    spare = jnp.zeros((SLOTS - heads, width), F32)
    for m in range(moves):
        pairs = asked_ref[slots[m]].astype(F32)
        query = [pairs[:, i * width : (i + 1) * width] for i in range(heads // 2)]
        query = jnp.concatenate(query + [spare], axis=0).astype(BF16)
        score_ref[m] = lax.dot_general(
            query, key_ref[pages[m]], NT, preferred_element_type=F32
        )
    scores = score_ref[...] * scale
    highest = jnp.max(scores, axis=-1, keepdims=True)
    weights = jnp.exp2(scores - highest)
    sums = jnp.sum(weights, axis=-1, keepdims=True)
    level = jnp.broadcast_to(highest + jnp.log(sums) * LOG2E, scores.shape)
    row = lax.broadcasted_iota(jnp.int32, scores.shape, 1)
    lane = lax.broadcasted_iota(jnp.int32, scores.shape, 2)
    level = jnp.sum(
        jnp.where((lane % SLOTS == row) & (row < heads), level, 0.0), axis=1, keepdims=True
    )
    first, second, third = split_three(jnp.broadcast_to(level, scores.shape))
    part = lane // SLOTS
    stats = jnp.where(part == 0, first, jnp.where(part == 1, second, third))
    inverse = 1.0 / sums
    rounded = weights.astype(BF16)
    out_ref[...] = jnp.zeros(out_ref.shape, out_ref.dtype)
    for m in range(moves):
        product = jnp.dot(rounded[m], value_ref[pages[m]], preferred_element_type=F32)
        product = product * inverse[m]
        message = jnp.where(row[m] < heads, product, stats[m])
        out_ref[slots[m]] = message.astype(BF16)


def local_kernel(scale, first, query_ref, key_ref, value_ref, table_ref, length_ref, *rest):
    out_ref, stat_ref, score_ref = rest[-3:]
    heads, requests, width = out_ref.shape
    heads = heads - first
    pool, page_len, _ = key_ref.shape
    pairs = pool // 2
    span = 2 * page_len
    lengths = length_ref[...]
    page = lax.broadcasted_iota(jnp.int32, (pool, requests), 0)
    counts = jnp.zeros((pool, requests), jnp.int32)
    for i in range(table_ref.shape[0]):
        held = jnp.clip(lengths - i * page_len, 0, page_len)
        counts = counts + jnp.where(table_ref[i : i + 1, :] == page, held, 0)
    token = lax.broadcasted_iota(jnp.int32, (page_len, requests), 0)
    query = query_ref[first : first + heads].reshape(heads * requests, width)
    lanes = [slice(h * requests, (h + 1) * requests) for h in range(heads)]
    best = [jnp.full((8, requests), FLOOR, F32)] * heads
    for p in range(pairs):
        keys = key_ref[2 * p : 2 * p + 2].reshape(span, width)
        scores = lax.dot_general(keys, query, NT, preferred_element_type=F32)
        usable = [token < counts[2 * p + i : 2 * p + i + 1] for i in range(2)]
        usable = jnp.concatenate(usable, axis=0)
        for h in range(heads):
            masked = jnp.where(usable, scores[:, lanes[h]] * scale, FLOOR)
            score_ref[p, :, lanes[h]] = masked
            best[h] = jnp.maximum(best[h], jnp.max(masked.reshape(span // 8, 8, requests), axis=0))
    best = jnp.concatenate([jnp.max(b, axis=0, keepdims=True) for b in best], axis=1)
    total = jnp.zeros((8, heads * requests), F32)
    out = jnp.zeros((width, heads * requests), F32)
    for p in range(pairs):
        weights = jnp.exp2(score_ref[p] - best)
        total = total + jnp.sum(weights.reshape(span // 8, 8, heads * requests), axis=0)
        values = value_ref[2 * p : 2 * p + 2].reshape(span, width)
        out = out + lax.dot_general(values, weights.astype(BF16), TN, preferred_element_type=F32)
    total = jnp.sum(total, axis=0, keepdims=True)
    if first:
        out_ref[:first] = rest[0][...]
        stat_ref[...] = rest[1][...]
    else:
        stat_ref[...] = jnp.zeros(stat_ref.shape, F32)
    for h in range(heads):
        out_ref[first + h] = out[:, lanes[h]].T
        stat_ref[first + h : first + h + 1] = best[:, lanes[h]]
        stat_ref[SLOTS + first + h : SLOTS + first + h + 1] = total[:, lanes[h]]


def norm_kernel(hidden_ref, gain_ref, _, scaled_ref, extra_ref):
    widened = hidden_ref[...].astype(F32)
    requests = widened.shape[0]
    scaled_ref[...] = (widened * gain_ref[...].astype(F32).reshape(1, -1)).astype(BF16)
    squares = jnp.sum(widened * widened, axis=1, keepdims=True)
    row = lax.broadcasted_iota(jnp.int32, (requests, LANES), 0)
    lane = lax.broadcasted_iota(jnp.int32, (requests, LANES), 1)
    squares = jnp.sum(jnp.where(row == lane, squares, 0.0), axis=0, keepdims=True)
    first, second, third = split_three(squares)
    upper = jnp.concatenate([first, second], axis=1)
    lower = jnp.concatenate([third, jnp.zeros_like(third)], axis=1)
    place = lax.broadcasted_iota(jnp.int32, extra_ref.shape, 0) - 2 * lax.axis_index("tp")
    extra_ref[...] = jnp.where(place == 0, upper, jnp.where(place == 1, lower, 0.0))


def place():
    rank = lax.axis_index("tp")
    return rank // 4, rank % 2, rank // 2 % 2


def first_kernel(partial_ref, extra_ref, send_ref, keep_ref):
    _, _, near = place()
    rows = partial_ref.shape[1]
    for i in range(2):
        for j in range(2):
            keep_ref[i, j, :rows] = partial_ref[4 * i + 2 * near + j]
            keep_ref[i, j, rows:] = extra_ref[...]
            send_ref[i, j, :rows] = partial_ref[4 * i + 2 * (1 - near) + j].astype(BF16)
            send_ref[i, j, rows:] = extra_ref[...].astype(BF16)


def second_kernel(got_ref, kept_ref, _, send_ref, keep_ref):
    far, _, _ = place()
    keep_ref[...] = kept_ref[far] + got_ref[far].astype(F32)
    send_ref[...] = (kept_ref[1 - far] + got_ref[1 - far].astype(F32)).astype(BF16)


def third_kernel(got_ref, kept_ref, length_ref, frequency_ref, send_ref, last_ref, angle_ref):
    _, side, _ = place()
    last_ref[...] = kept_ref[side] + got_ref[side].astype(F32)
    send_ref[...] = (kept_ref[1 - side] + got_ref[1 - side].astype(F32)).astype(BF16)
    requests, half = angle_ref.shape
    lengths = jnp.broadcast_to(length_ref[...].astype(F32), (LANES, requests)).T
    angle_ref[...] = lengths[:, :half] * frequency_ref[...]


def fresh_kernel(scale, features, got_ref, last_ref, cos_ref, sin_ref, query_ref, kv_ref, score_ref):
    heads, requests, width = query_ref.shape
    total = last_ref[...] + got_ref[...].astype(F32)
    extra = jnp.sum(total[requests:], axis=0, keepdims=True)
    squares = extra[:, :LANES] + extra[:, LANES:]
    row = lax.broadcasted_iota(jnp.int32, (requests, LANES), 0)
    lane = lax.broadcasted_iota(jnp.int32, (requests, LANES), 1)
    squares = jnp.sum(jnp.where(row == lane, squares, 0.0), axis=1, keepdims=True)
    inverse = lax.rsqrt(squares / features + EPSILON)
    projected = total[:requests] * inverse
    key = projected[:, :width]
    key = key * cos_ref[...] + pltpu.roll(key, width // 2, 1) * sin_ref[...]
    key = key.astype(BF16)
    kv_ref[:, :width] = key
    kv_ref[:, width:] = projected[:, width:].astype(BF16)
    key = key.astype(F32)
    scores = jnp.zeros((requests, LANES), F32)
    for h in range(heads):
        score = jnp.sum(query_ref[h].astype(F32) * key, axis=1, keepdims=True)
        scores = jnp.where(lane == h, score * scale, scores)
    score_ref[...] = scores.T[:SLOTS]


def owner_kernel(label_ref, owner_ref):
    slots, requests = owner_ref.shape
    labels = label_ref[...].reshape(slots, LANES)
    owner_ref[...] = jnp.where(
        labels == lax.broadcasted_iota(jnp.int32, (slots, requests), 1), 0.0, FLOOR
    )


def combine_kernel(message_ref, owner_ref, out_ref, stat_ref, fresh_ref, kv_ref, final_ref, new_kv_ref):
    heads, requests, width = out_ref.shape
    messages = jnp.swapaxes(message_ref[...].astype(F32), 0, 1)
    levels = messages[heads]
    levels = levels[:, :SLOTS] + levels[:, SLOTS : 2 * SLOTS] + levels[:, 2 * SLOTS : 3 * SLOTS]
    owner = owner_ref[...]
    scores = [owner + levels[:, h : h + 1] for h in range(heads)]
    rows = [jnp.max(score, axis=0, keepdims=True) for score in scores]
    moved_best = jnp.concatenate(rows + [rows[0]] * (SLOTS - heads), axis=0)
    stats = stat_ref[...]
    highest = stats[:SLOTS]
    fresh = fresh_ref[...]
    best = jnp.maximum(jnp.maximum(highest, fresh), moved_best)
    weights = [jnp.exp2(scores[h] - best[h : h + 1]) for h in range(heads)]
    rows = [jnp.sum(weight, axis=0, keepdims=True) for weight in weights]
    moved_sums = jnp.concatenate(rows + [rows[0]] * (SLOTS - heads), axis=0)
    factor = jnp.exp2(highest - best)
    fresh = jnp.exp2(fresh - best)
    inverse = 1.0 / (stats[SLOTS:] * factor + fresh + moved_sums)
    columns = jnp.concatenate(
        [factor * inverse, fresh * inverse, jnp.zeros((LANES - 2 * SLOTS, requests), F32)], axis=0
    ).T
    new_kv_ref[...] = kv_ref[...]
    value = kv_ref[:, width:].astype(F32)
    for h in range(heads):
        weight = weights[h] * inverse[h : h + 1]
        coarse = weight.astype(BF16)
        fine = (weight - coarse.astype(F32)).astype(BF16)
        moved = messages[h].astype(BF16)
        total = lax.dot_general(
            jnp.concatenate([coarse, fine], axis=0),
            jnp.concatenate([moved, moved], axis=0),
            TN,
            preferred_element_type=F32,
        )
        total = total + out_ref[h] * columns[:, h : h + 1] + value * columns[:, SLOTS + h : SLOTS + h + 1]
        final_ref[:, h * width : (h + 1) * width] = total.astype(BF16)


def call(kernel, shapes, ins, scratch=(), limit=8, flops=10**9, moved=0):
    return pl.pallas_call(
        kernel,
        out_shape=shapes,
        in_specs=ins,
        out_specs=jax.tree.map(lambda _: VMEM, shapes),
        scratch_shapes=scratch,
        compiler_params=pltpu.CompilerParams(vmem_limit_bytes=limit * 1024 * 1024),
        cost_estimate=pl.CostEstimate(flops=flops, bytes_accessed=moved, transcendentals=0),
    )


def frequencies(width):
    steps = jnp.arange(width // 2, dtype=F32)
    return (ROPE_BASE ** (-2.0 * steps / width))[None, :]


def body(
    hidden_state,
    norm_gain,
    kv_weight,
    queries,
    pool_keys,
    pool_values,
    page_table,
    lengths,
    move_target,
    move_page,
    move_request,
):
    shape = jax.ShapeDtypeStruct
    requests, heads, width = queries.shape
    pool, _, page_len, _ = pool_keys.shape
    moves = move_page.shape[0]
    instances = lax.axis_size("inst")
    ranks = lax.axis_size("tp")
    features = hidden_state.shape[1] * ranks
    scale = LOG2E / math.sqrt(width)
    root = instances * 26 // 32
    order = [(i + root) % instances for i in range(instances)]

    def exchange(x):
        return lax.all_to_all(x, "inst", 0, 0, tiled=True, axis_index_groups=[order])


    def swap(x, bit):
        return lax.ppermute(x, "tp", [(i, i ^ bit) for i in range(ranks)])

    keys = pool_keys.reshape(pool, page_len, width)
    values = pool_values.reshape(pool, page_len, width)
    by_head = jnp.transpose(queries, (1, 0, 2))

    bits = ((requests - 1).bit_length(), (pool - 1).bit_length())
    plan = (((move_target[:, 0] << bits[0]) | move_request) << bits[1]) | move_page
    labels = call(
        functools.partial(label_kernel, bits, root),
        shape((instances, 1, LANES), jnp.int32),
        [VMEM],
        flops=10**10,
    )(plan.reshape(1, moves))
    labels = exchange(labels)

    scaled, extra = call(
        norm_kernel,
        [shape(hidden_state.shape, BF16), shape((16, 2 * width), F32)],
        [VMEM, VMEM, ANY],
    )(hidden_state, norm_gain, kv_weight)
    partial = jnp.einsum("rf,fgc->grc", scaled, kv_weight, preferred_element_type=F32)
    padded = requests + 16
    send, keep = call(
        first_kernel,
        [shape((2, 2, padded, 2 * width), BF16), shape((2, 2, padded, 2 * width), F32)],
        [VMEM, VMEM],
    )(partial, extra)
    got = swap(send, 2)

    def local(first, stop, cost, *earlier):
        return call(
            functools.partial(local_kernel, scale, first),
            [shape((stop, requests, width), F32), shape((2 * SLOTS, requests), F32)],
            [VMEM] * 5 + [VMEM, VMEM, ANY][: len(earlier)],
            [pltpu.VMEM((pool // 2, 2 * page_len, (stop - first) * requests), F32)],
            limit=16,
            flops=cost,
        )(by_head, keys, values, page_table.T, lengths[None, :], *earlier)

    asked = call(ask_kernel, shape((instances, 2, heads // 2 * width), BF16), [VMEM, VMEM, ANY])(labels, by_head, send)
    asked = exchange(asked)

    out, stats = local(0, heads // 2, 3 * 10**9)
    send, keep = call(
        second_kernel,
        [shape((2, padded, 2 * width), BF16), shape((2, padded, 2 * width), F32)],
        [VMEM, VMEM, ANY],
        flops=SECOND,
    )(got, keep, stats)
    got = swap(send, 4)

    answers = call(
        functools.partial(moved_kernel, scale, heads, bits, root),
        shape((instances, SLOTS, width), BF16),
        [VMEM, VMEM, VMEM, VMEM, ANY],
        [pltpu.VMEM((moves, SLOTS, page_len), F32)],
    )(plan.reshape(1, moves), asked, keys, values, send)
    answers = exchange(answers)

    owner = call(
        owner_kernel, shape((instances, requests), F32), [VMEM], flops=0
    )(labels)
    send, last, angles = call(
        third_kernel,
        [
            shape((padded, 2 * width), BF16),
            shape((padded, 2 * width), F32),
            shape((requests, width // 2), F32),
        ],
        [VMEM] * 4,
        flops=THIRD,
    )(got, keep, lengths[None, :], frequencies(width))
    out, stats = local(heads // 2, heads, LATER, out, stats, send)
    got = swap(send, 1)
    cosine = jnp.cos(angles)
    sine = jnp.sin(angles)
    cosine = jnp.concatenate([cosine, cosine], axis=1)
    sine = jnp.concatenate([-sine, sine], axis=1)
    kv, fresh = call(
        functools.partial(fresh_kernel, scale, features),
        [shape((requests, 2 * width), BF16), shape((SLOTS, requests), F32)],
        [VMEM] * 5,
    )(got, last, cosine, sine, by_head)
    attention_out, new_kv = call(
        combine_kernel,
        [shape((requests, heads * width), BF16), shape((requests, 2 * width), BF16)],
        [VMEM] * 6,
    )(answers, owner, out, stats, fresh, kv)
    return (attention_out, new_kv.reshape(requests, 1, 2 * width))


def solution(mesh):
    return jax.shard_map(
        body,
        mesh=mesh,
        in_specs=(
            P("inst", "tp"),
            P("tp"),
            P("tp", None, None),
            P("inst", "tp", None),
            P("inst", "tp", None, None),
            P("inst", "tp", None, None),
            P("inst", None),
            P("inst"),
            P("inst", None),
            P("inst"),
            P("inst"),
        ),
        out_specs=(P("inst", "tp"), P("inst", "tp", None)),
        check_vma=False,
    )
```

```python
import functools
import math

import jax
import jax.numpy as jnp
from jax import lax
from jax.experimental import pallas as pl
from jax.experimental.pallas import tpu as pltpu
from jax.sharding import PartitionSpec as P

EPSILON = 1e-05
ROPE_BASE = 1000000.0
FLOOR = -1e30
SECOND = 0
THIRD = 10**9
LATER = 2 * 10**8
LANES = 128
SLOTS = 8
LOG2E = 1.4426950408889634
VMEM = pl.BlockSpec(memory_space=pltpu.VMEM)
SMEM = pl.BlockSpec(memory_space=pltpu.SMEM)
ANY = pl.BlockSpec(memory_space=pl.ANY)
HBM = pl.BlockSpec(memory_space=pltpu.HBM)
F32 = jnp.float32
BF16 = jnp.bfloat16
NT = (((1,), (1,)), ((), ()))
TN = (((0,), (0,)), ((), ()))


def split_three(x):
    first = x.astype(BF16).astype(F32)
    second = (x - first).astype(BF16).astype(F32)
    third = (x - first - second).astype(BF16).astype(F32)
    return first, second, third


def slot_of(code, bits, root, slots):
    return lax.rem((code >> sum(bits)) + (slots - root), slots)


def label_kernel(bits, root, plan_ref, label_ref):
    slots = label_ref.shape[0]
    plan = plan_ref[...]
    place = slot_of(plan, bits, root, slots)
    request = (plan >> bits[1]) & ((1 << bits[0]) - 1)
    named = place == lax.broadcasted_iota(jnp.int32, (slots, plan.shape[1]), 0)
    found = jnp.sum(jnp.where(named, request + 1, 0), axis=1, keepdims=True) - 1
    label_ref[...] = jnp.broadcast_to(found, (slots, LANES)).reshape(slots, 1, LANES)


def ask_kernel(label_ref, query_ref, *rest):
    asked_ref = rest[-1]
    heads, requests, width = query_ref.shape
    slots = asked_ref.shape[0]
    labels = label_ref[...].reshape(slots, LANES)
    chosen = labels == lax.broadcasted_iota(jnp.int32, (slots, requests), 1)
    chosen = jnp.where(chosen, 1.0, 0.0).astype(BF16)
    rows = [jnp.dot(chosen, query_ref[h], preferred_element_type=F32) for h in range(heads)]
    halves = [jnp.concatenate(rows[i::2], axis=1) for i in range(2)]
    asked_ref[...] = jnp.swapaxes(jnp.stack(halves), 0, 1).astype(BF16)


def moved_kernel(scale, heads, bits, root, plan_ref, asked_ref, key_ref, value_ref, *rest):
    out_ref, score_ref = rest[-2:]
    moves = plan_ref.shape[1]
    width = out_ref.shape[2]
    plan = [plan_ref[0, m] for m in range(moves)]
    slots = [slot_of(code, bits, root, out_ref.shape[0]) for code in plan]
    pages = [code & ((1 << bits[1]) - 1) for code in plan]
    page_len = key_ref.shape[1]
    couples = [(m, min(m + 1, moves - 1)) for m in range(0, moves, 2)]
    spare = jnp.zeros((SLOTS - heads, width), F32)
    for couple in couples:
        query = []
        for m in couple:
            pairs = asked_ref[slots[m]].astype(F32)
            query += [pairs[:, i * width : (i + 1) * width] for i in range(heads // 2)] + [spare]
        query = jnp.concatenate(query, axis=0).astype(BF16)
        keys = jnp.concatenate([key_ref[pages[m]] for m in couple], axis=0)
        product = lax.dot_general(query, keys, NT, preferred_element_type=F32)
        for i, m in enumerate(couple):
            score_ref[m] = product[i * SLOTS : (i + 1) * SLOTS, i * page_len : (i + 1) * page_len]
    scores = score_ref[...] * scale
    highest = jnp.max(scores, axis=-1, keepdims=True)
    weights = jnp.exp2(scores - highest)
    sums = jnp.sum(weights, axis=-1, keepdims=True)
    level = jnp.broadcast_to(highest + jnp.log(sums) * LOG2E, scores.shape)
    row = lax.broadcasted_iota(jnp.int32, scores.shape, 1)
    lane = lax.broadcasted_iota(jnp.int32, scores.shape, 2)
    level = jnp.sum(
        jnp.where((lane % SLOTS == row) & (row < heads), level, 0.0), axis=1, keepdims=True
    )
    first, second, third = split_three(jnp.broadcast_to(level, scores.shape))
    part = lane // SLOTS
    stats = jnp.where(part == 0, first, jnp.where(part == 1, second, third))
    inverse = 1.0 / sums
    out_ref[...] = jnp.zeros(out_ref.shape, out_ref.dtype)
    blank = jnp.zeros((SLOTS, page_len), F32)
    for one, other in couples:
        spread = [
            jnp.concatenate([weights[one], blank], axis=1),
            jnp.concatenate([blank, weights[other]], axis=1),
        ]
        spread = jnp.concatenate(spread, axis=0).astype(BF16)
        values = jnp.concatenate([value_ref[pages[one]], value_ref[pages[other]]], axis=0)
        product = jnp.dot(spread, values, preferred_element_type=F32)
        for i, m in enumerate((one, other)):
            part_out = product[i * SLOTS : (i + 1) * SLOTS] * inverse[m]
            out_ref[slots[m]] = jnp.where(row[m] < heads, part_out, stats[m]).astype(BF16)


def local_kernel(scale, first, query_ref, key_ref, value_ref, table_ref, length_ref, *rest):
    out_ref, stat_ref, score_ref = rest[-3:]
    heads, requests, width = out_ref.shape
    heads = heads - first
    pool, page_len, _ = key_ref.shape
    pairs = pool // 2
    span = 2 * page_len
    lengths = length_ref[...]
    page = lax.broadcasted_iota(jnp.int32, (pool, requests), 0)
    counts = jnp.zeros((pool, requests), jnp.int32)
    for i in range(table_ref.shape[0]):
        held = jnp.clip(lengths - i * page_len, 0, page_len)
        counts = counts + jnp.where(table_ref[i : i + 1, :] == page, held, 0)
    token = lax.broadcasted_iota(jnp.int32, (page_len, requests), 0)
    query = query_ref[first : first + heads].reshape(heads * requests, width)
    lanes = [slice(h * requests, (h + 1) * requests) for h in range(heads)]
    best = [jnp.full((8, requests), FLOOR, F32)] * heads
    for p in range(pairs):
        keys = key_ref[2 * p : 2 * p + 2].reshape(span, width)
        scores = lax.dot_general(keys, query, NT, preferred_element_type=F32)
        usable = [token < counts[2 * p + i : 2 * p + i + 1] for i in range(2)]
        usable = jnp.concatenate(usable, axis=0)
        for h in range(heads):
            masked = jnp.where(usable, scores[:, lanes[h]] * scale, FLOOR)
            score_ref[p, :, lanes[h]] = masked
            best[h] = jnp.maximum(best[h], jnp.max(masked.reshape(span // 8, 8, requests), axis=0))
    best = jnp.concatenate([jnp.max(b, axis=0, keepdims=True) for b in best], axis=1)
    total = jnp.zeros((8, heads * requests), F32)
    out = jnp.zeros((width, heads * requests), F32)
    for p in range(pairs):
        weights = jnp.exp2(score_ref[p] - best)
        total = total + jnp.sum(weights.reshape(span // 8, 8, heads * requests), axis=0)
        values = value_ref[2 * p : 2 * p + 2].reshape(span, width)
        out = out + lax.dot_general(values, weights.astype(BF16), TN, preferred_element_type=F32)
    total = jnp.sum(total, axis=0, keepdims=True)
    if first:
        out_ref[:first] = rest[0][...]
        stat_ref[...] = rest[1][...]
    else:
        stat_ref[...] = jnp.zeros(stat_ref.shape, F32)
    for h in range(heads):
        out_ref[first + h] = out[:, lanes[h]].T
        stat_ref[first + h : first + h + 1] = best[:, lanes[h]]
        stat_ref[SLOTS + first + h : SLOTS + first + h + 1] = total[:, lanes[h]]


def norm_kernel(hidden_ref, gain_ref, _, scaled_ref, extra_ref):
    widened = hidden_ref[...].astype(F32)
    requests = widened.shape[0]
    scaled_ref[...] = (widened * gain_ref[...].astype(F32).reshape(1, -1)).astype(BF16)
    squares = jnp.sum(widened * widened, axis=1, keepdims=True)
    row = lax.broadcasted_iota(jnp.int32, (requests, LANES), 0)
    lane = lax.broadcasted_iota(jnp.int32, (requests, LANES), 1)
    squares = jnp.sum(jnp.where(row == lane, squares, 0.0), axis=0, keepdims=True)
    first, second, third = split_three(squares)
    upper = jnp.concatenate([first, second], axis=1)
    lower = jnp.concatenate([third, jnp.zeros_like(third)], axis=1)
    place = lax.broadcasted_iota(jnp.int32, extra_ref.shape, 0) - 2 * lax.axis_index("tp")
    extra_ref[...] = jnp.where(place == 0, upper, jnp.where(place == 1, lower, 0.0))


def place():
    rank = lax.axis_index("tp")
    return rank // 4, rank % 2, rank // 2 % 2


def first_kernel(partial_ref, extra_ref, send_ref, keep_ref):
    _, _, near = place()
    rows = partial_ref.shape[1]
    for i in range(2):
        for j in range(2):
            keep_ref[i, j, :rows] = partial_ref[4 * i + 2 * near + j]
            keep_ref[i, j, rows:] = extra_ref[...]
            send_ref[i, j, :rows] = partial_ref[4 * i + 2 * (1 - near) + j].astype(BF16)
            send_ref[i, j, rows:] = extra_ref[...].astype(BF16)


def second_kernel(got_ref, kept_ref, _, send_ref, keep_ref):
    far, _, _ = place()
    keep_ref[...] = kept_ref[far] + got_ref[far].astype(F32)
    send_ref[...] = (kept_ref[1 - far] + got_ref[1 - far].astype(F32)).astype(BF16)


def third_kernel(got_ref, kept_ref, length_ref, frequency_ref, send_ref, last_ref, angle_ref):
    _, side, _ = place()
    last_ref[...] = kept_ref[side] + got_ref[side].astype(F32)
    send_ref[...] = (kept_ref[1 - side] + got_ref[1 - side].astype(F32)).astype(BF16)
    requests, half = angle_ref.shape
    lengths = jnp.broadcast_to(length_ref[...].astype(F32), (LANES, requests)).T
    angle_ref[...] = lengths[:, :half] * frequency_ref[...]


def fresh_kernel(scale, features, got_ref, last_ref, cos_ref, sin_ref, query_ref, kv_ref, score_ref):
    heads, requests, width = query_ref.shape
    total = last_ref[...] + got_ref[...].astype(F32)
    extra = jnp.sum(total[requests:], axis=0, keepdims=True)
    squares = extra[:, :LANES] + extra[:, LANES:]
    row = lax.broadcasted_iota(jnp.int32, (requests, LANES), 0)
    lane = lax.broadcasted_iota(jnp.int32, (requests, LANES), 1)
    squares = jnp.sum(jnp.where(row == lane, squares, 0.0), axis=1, keepdims=True)
    inverse = lax.rsqrt(squares / features + EPSILON)
    projected = total[:requests] * inverse
    key = projected[:, :width]
    key = key * cos_ref[...] + pltpu.roll(key, width // 2, 1) * sin_ref[...]
    key = key.astype(BF16)
    kv_ref[:, :width] = key
    kv_ref[:, width:] = projected[:, width:].astype(BF16)
    key = key.astype(F32)
    scores = jnp.zeros((requests, LANES), F32)
    for h in range(heads):
        score = jnp.sum(query_ref[h].astype(F32) * key, axis=1, keepdims=True)
        scores = jnp.where(lane == h, score * scale, scores)
    score_ref[...] = scores.T[:SLOTS]


def owner_kernel(label_ref, owner_ref):
    slots, requests = owner_ref.shape
    labels = label_ref[...].reshape(slots, LANES)
    owner_ref[...] = jnp.where(
        labels == lax.broadcasted_iota(jnp.int32, (slots, requests), 1), 0.0, FLOOR
    )


def combine_kernel(message_ref, owner_ref, out_ref, stat_ref, fresh_ref, kv_ref, final_ref, new_kv_ref):
    heads, requests, width = out_ref.shape
    messages = jnp.swapaxes(message_ref[...].astype(F32), 0, 1)
    levels = messages[heads]
    levels = levels[:, :SLOTS] + levels[:, SLOTS : 2 * SLOTS] + levels[:, 2 * SLOTS : 3 * SLOTS]
    owner = owner_ref[...]
    scores = [owner + levels[:, h : h + 1] for h in range(heads)]
    rows = [jnp.max(score, axis=0, keepdims=True) for score in scores]
    moved_best = jnp.concatenate(rows + [rows[0]] * (SLOTS - heads), axis=0)
    stats = stat_ref[...]
    highest = stats[:SLOTS]
    fresh = fresh_ref[...]
    best = jnp.maximum(jnp.maximum(highest, fresh), moved_best)
    weights = [jnp.exp2(scores[h] - best[h : h + 1]) for h in range(heads)]
    rows = [jnp.sum(weight, axis=0, keepdims=True) for weight in weights]
    moved_sums = jnp.concatenate(rows + [rows[0]] * (SLOTS - heads), axis=0)
    factor = jnp.exp2(highest - best)
    fresh = jnp.exp2(fresh - best)
    inverse = 1.0 / (stats[SLOTS:] * factor + fresh + moved_sums)
    columns = jnp.concatenate(
        [factor * inverse, fresh * inverse, jnp.zeros((LANES - 2 * SLOTS, requests), F32)], axis=0
    ).T
    new_kv_ref[...] = kv_ref[...]
    value = kv_ref[:, width:].astype(F32)
    for h in range(heads):
        weight = weights[h] * inverse[h : h + 1]
        coarse = weight.astype(BF16)
        fine = (weight - coarse.astype(F32)).astype(BF16)
        moved = messages[h].astype(BF16)
        total = lax.dot_general(
            jnp.concatenate([coarse, fine], axis=0),
            jnp.concatenate([moved, moved], axis=0),
            TN,
            preferred_element_type=F32,
        )
        total = total + out_ref[h] * columns[:, h : h + 1] + value * columns[:, SLOTS + h : SLOTS + h + 1]
        final_ref[:, h * width : (h + 1) * width] = total.astype(BF16)


def call(kernel, shapes, ins, scratch=(), limit=8, flops=10**9, moved=0):
    return pl.pallas_call(
        kernel,
        out_shape=shapes,
        in_specs=ins,
        out_specs=jax.tree.map(lambda _: VMEM, shapes),
        scratch_shapes=scratch,
        compiler_params=pltpu.CompilerParams(vmem_limit_bytes=limit * 1024 * 1024),
        cost_estimate=pl.CostEstimate(flops=flops, bytes_accessed=moved, transcendentals=0),
    )


def frequencies(width):
    steps = jnp.arange(width // 2, dtype=F32)
    return (ROPE_BASE ** (-2.0 * steps / width))[None, :]


def body(
    hidden_state,
    norm_gain,
    kv_weight,
    queries,
    pool_keys,
    pool_values,
    page_table,
    lengths,
    move_target,
    move_page,
    move_request,
):
    shape = jax.ShapeDtypeStruct
    requests, heads, width = queries.shape
    pool, _, page_len, _ = pool_keys.shape
    moves = move_page.shape[0]
    instances = lax.axis_size("inst")
    ranks = lax.axis_size("tp")
    features = hidden_state.shape[1] * ranks
    scale = LOG2E / math.sqrt(width)
    root = instances * 26 // 32
    order = [(i + root) % instances for i in range(instances)]

    def exchange(x):
        return lax.all_to_all(x, "inst", 0, 0, tiled=True, axis_index_groups=[order])


    def swap(x, bit):
        return lax.ppermute(x, "tp", [(i, i ^ bit) for i in range(ranks)])

    keys = pool_keys.reshape(pool, page_len, width)
    values = pool_values.reshape(pool, page_len, width)
    by_head = jnp.transpose(queries, (1, 0, 2))

    bits = ((requests - 1).bit_length(), (pool - 1).bit_length())
    plan = (((move_target[:, 0] << bits[0]) | move_request) << bits[1]) | move_page
    labels = call(
        functools.partial(label_kernel, bits, root),
        shape((instances, 1, LANES), jnp.int32),
        [VMEM],
        flops=10**10,
    )(plan.reshape(1, moves))
    labels = exchange(labels)

    scaled, extra = call(
        norm_kernel,
        [shape(hidden_state.shape, BF16), shape((16, 2 * width), F32)],
        [VMEM, VMEM, ANY],
    )(hidden_state, norm_gain, kv_weight)
    partial = jnp.einsum("rf,fgc->grc", scaled, kv_weight, preferred_element_type=F32)
    padded = requests + 16
    send, keep = call(
        first_kernel,
        [shape((2, 2, padded, 2 * width), BF16), shape((2, 2, padded, 2 * width), F32)],
        [VMEM, VMEM],
    )(partial, extra)
    got = swap(send, 2)

    def local(first, stop, cost, *earlier):
        return call(
            functools.partial(local_kernel, scale, first),
            [shape((stop, requests, width), F32), shape((2 * SLOTS, requests), F32)],
            [VMEM] * 5 + [VMEM, VMEM, ANY][: len(earlier)],
            [pltpu.VMEM((pool // 2, 2 * page_len, (stop - first) * requests), F32)],
            limit=16,
            flops=cost,
        )(by_head, keys, values, page_table.T, lengths[None, :], *earlier)

    asked = call(ask_kernel, shape((instances, 2, heads // 2 * width), BF16), [VMEM, VMEM, ANY])(labels, by_head, send)
    asked = exchange(asked)

    out, stats = local(0, heads // 2, 3 * 10**9)
    send, keep = call(
        second_kernel,
        [shape((2, padded, 2 * width), BF16), shape((2, padded, 2 * width), F32)],
        [VMEM, VMEM, ANY],
        flops=SECOND,
    )(got, keep, stats)
    got = swap(send, 4)

    answers = call(
        functools.partial(moved_kernel, scale, heads, bits, root),
        shape((instances, SLOTS, width), BF16),
        [VMEM, VMEM, VMEM, VMEM, ANY],
        [pltpu.VMEM((moves, SLOTS, page_len), F32)],
    )(plan.reshape(1, moves), asked, keys, values, send)
    answers = exchange(answers)

    owner = call(
        owner_kernel, shape((instances, requests), F32), [VMEM], flops=0
    )(labels)
    send, last, angles = call(
        third_kernel,
        [
            shape((padded, 2 * width), BF16),
            shape((padded, 2 * width), F32),
            shape((requests, width // 2), F32),
        ],
        [VMEM] * 4,
        flops=THIRD,
    )(got, keep, lengths[None, :], frequencies(width))
    out, stats = local(heads // 2, heads, LATER, out, stats, send)
    got = swap(send, 1)
    cosine = jnp.cos(angles)
    sine = jnp.sin(angles)
    cosine = jnp.concatenate([cosine, cosine], axis=1)
    sine = jnp.concatenate([-sine, sine], axis=1)
    kv, fresh = call(
        functools.partial(fresh_kernel, scale, features),
        [shape((requests, 2 * width), BF16), shape((SLOTS, requests), F32)],
        [VMEM] * 5,
    )(got, last, cosine, sine, by_head)
    attention_out, new_kv = call(
        combine_kernel,
        [shape((requests, heads * width), BF16), shape((requests, 2 * width), BF16)],
        [VMEM] * 6,
    )(answers, owner, out, stats, fresh, kv)
    return (attention_out, new_kv.reshape(requests, 1, 2 * width))


def solution(mesh):
    return jax.shard_map(
        body,
        mesh=mesh,
        in_specs=(
            P("inst", "tp"),
            P("tp"),
            P("tp", None, None),
            P("inst", "tp", None),
            P("inst", "tp", None, None),
            P("inst", "tp", None, None),
            P("inst", None),
            P("inst"),
            P("inst", None),
            P("inst"),
            P("inst"),
        ),
        out_specs=(P("inst", "tp"), P("inst", "tp", None)),
        check_vma=False,
    )
```

```python
import functools
import math

import jax
import jax.numpy as jnp
from jax import lax
from jax.experimental import pallas as pl
from jax.experimental.pallas import tpu as pltpu
from jax.sharding import PartitionSpec as P

EPSILON = 1e-05
ROPE_BASE = 1000000.0
FLOOR = -1e30
SECOND = 0
THIRD = 10**9
LATER = 2 * 10**8
LANES = 128
SLOTS = 8
LOG2E = 1.4426950408889634
VMEM = pl.BlockSpec(memory_space=pltpu.VMEM)
SMEM = pl.BlockSpec(memory_space=pltpu.SMEM)
ANY = pl.BlockSpec(memory_space=pl.ANY)
HBM = pl.BlockSpec(memory_space=pltpu.HBM)
F32 = jnp.float32
BF16 = jnp.bfloat16
NT = (((1,), (1,)), ((), ()))
TN = (((0,), (0,)), ((), ()))


def split_three(x):
    first = x.astype(BF16).astype(F32)
    second = (x - first).astype(BF16).astype(F32)
    third = (x - first - second).astype(BF16).astype(F32)
    return first, second, third


def slot_of(code, bits, root, slots):
    return lax.rem((code >> sum(bits)) + (slots - root), slots)


def label_kernel(bits, root, plan_ref, label_ref):
    slots = label_ref.shape[0]
    plan = plan_ref[...]
    place = slot_of(plan, bits, root, slots)
    request = (plan >> bits[1]) & ((1 << bits[0]) - 1)
    named = place == lax.broadcasted_iota(jnp.int32, (slots, plan.shape[1]), 0)
    found = jnp.sum(jnp.where(named, request + 1, 0), axis=1, keepdims=True) - 1
    label_ref[...] = jnp.broadcast_to(found, (slots, LANES)).reshape(slots, 1, LANES)


def ask_kernel(label_ref, query_ref, *rest):
    asked_ref = rest[-1]
    heads, requests, width = query_ref.shape
    slots = asked_ref.shape[0]
    labels = label_ref[...].reshape(slots, LANES)
    chosen = labels == lax.broadcasted_iota(jnp.int32, (slots, requests), 1)
    chosen = jnp.where(chosen, 1.0, 0.0).astype(BF16)
    rows = [jnp.dot(chosen, query_ref[h], preferred_element_type=F32) for h in range(heads)]
    halves = [jnp.concatenate(rows[i::2], axis=1) for i in range(2)]
    asked_ref[...] = jnp.swapaxes(jnp.stack(halves), 0, 1).astype(BF16)


def moved_kernel(scale, heads, bits, root, plan_ref, asked_ref, key_ref, value_ref, *rest):
    out_ref, score_ref = rest[-2:]
    moves = plan_ref.shape[1]
    width = out_ref.shape[2]
    plan = [plan_ref[0, m] for m in range(moves)]
    slots = [slot_of(code, bits, root, out_ref.shape[0]) for code in plan]
    pages = [code & ((1 << bits[1]) - 1) for code in plan]
    page_len = key_ref.shape[1]
    couples = [(m, min(m + 1, moves - 1)) for m in range(0, moves, 2)]
    spare = jnp.zeros((SLOTS - heads, width), F32)
    for couple in couples:
        query = []
        for m in couple:
            pairs = asked_ref[slots[m]].astype(F32)
            query += [pairs[:, i * width : (i + 1) * width] for i in range(heads // 2)] + [spare]
        query = jnp.concatenate(query, axis=0).astype(BF16)
        keys = jnp.concatenate([key_ref[pages[m]] for m in couple], axis=0)
        product = lax.dot_general(query, keys, NT, preferred_element_type=F32)
        for i, m in enumerate(couple):
            score_ref[m] = product[i * SLOTS : (i + 1) * SLOTS, i * page_len : (i + 1) * page_len]
    scores = score_ref[...] * scale
    highest = jnp.max(scores, axis=-1, keepdims=True)
    weights = jnp.exp2(scores - highest)
    sums = jnp.sum(weights, axis=-1, keepdims=True)
    level = jnp.broadcast_to(highest + jnp.log(sums) * LOG2E, scores.shape)
    row = lax.broadcasted_iota(jnp.int32, scores.shape, 1)
    lane = lax.broadcasted_iota(jnp.int32, scores.shape, 2)
    level = jnp.sum(
        jnp.where((lane % SLOTS == row) & (row < heads), level, 0.0), axis=1, keepdims=True
    )
    first, second, third = split_three(jnp.broadcast_to(level, scores.shape))
    part = lane // SLOTS
    stats = jnp.where(part == 0, first, jnp.where(part == 1, second, third))
    inverse = 1.0 / sums
    out_ref[...] = jnp.zeros(out_ref.shape, out_ref.dtype)
    blank = jnp.zeros((SLOTS, page_len), F32)
    for one, other in couples:
        spread = [
            jnp.concatenate([weights[one], blank], axis=1),
            jnp.concatenate([blank, weights[other]], axis=1),
        ]
        spread = jnp.concatenate(spread, axis=0).astype(BF16)
        values = jnp.concatenate([value_ref[pages[one]], value_ref[pages[other]]], axis=0)
        product = jnp.dot(spread, values, preferred_element_type=F32)
        for i, m in enumerate((one, other)):
            part_out = product[i * SLOTS : (i + 1) * SLOTS] * inverse[m]
            out_ref[slots[m]] = jnp.where(row[m] < heads, part_out, stats[m]).astype(BF16)


def local_kernel(scale, first, query_ref, key_ref, value_ref, table_ref, length_ref, *rest):
    out_ref, stat_ref, score_ref = rest[-3:]
    heads, requests, width = out_ref.shape
    heads = heads - first
    pool, page_len, _ = key_ref.shape
    pairs = pool // 2
    span = 2 * page_len
    lengths = length_ref[...]
    page = lax.broadcasted_iota(jnp.int32, (pool, requests), 0)
    counts = jnp.zeros((pool, requests), jnp.int32)
    for i in range(table_ref.shape[0]):
        held = jnp.clip(lengths - i * page_len, 0, page_len)
        counts = counts + jnp.where(table_ref[i : i + 1, :] == page, held, 0)
    token = lax.broadcasted_iota(jnp.int32, (page_len, requests), 0)
    query = query_ref[first : first + heads].reshape(heads * requests, width)
    lanes = [slice(h * requests, (h + 1) * requests) for h in range(heads)]
    best = [jnp.full((8, requests), FLOOR, F32)] * heads
    for p in range(pairs):
        keys = key_ref[2 * p : 2 * p + 2].reshape(span, width)
        scores = lax.dot_general(keys, query, NT, preferred_element_type=F32)
        usable = [token < counts[2 * p + i : 2 * p + i + 1] for i in range(2)]
        usable = jnp.concatenate(usable, axis=0)
        for h in range(heads):
            masked = jnp.where(usable, scores[:, lanes[h]] * scale, FLOOR)
            score_ref[p, :, lanes[h]] = masked
            best[h] = jnp.maximum(best[h], jnp.max(masked.reshape(span // 8, 8, requests), axis=0))
    best = jnp.concatenate([jnp.max(b, axis=0, keepdims=True) for b in best], axis=1)
    total = jnp.zeros((8, heads * requests), F32)
    out = jnp.zeros((width, heads * requests), F32)
    for p in range(pairs):
        weights = jnp.exp2(score_ref[p] - best)
        total = total + jnp.sum(weights.reshape(span // 8, 8, heads * requests), axis=0)
        values = value_ref[2 * p : 2 * p + 2].reshape(span, width)
        out = out + lax.dot_general(values, weights.astype(BF16), TN, preferred_element_type=F32)
    total = jnp.sum(total, axis=0, keepdims=True)
    if first:
        out_ref[:first] = rest[0][...]
        stat_ref[...] = rest[1][...]
    else:
        stat_ref[...] = jnp.zeros(stat_ref.shape, F32)
    for h in range(heads):
        out_ref[first + h] = out[:, lanes[h]].T
        stat_ref[first + h : first + h + 1] = best[:, lanes[h]]
        stat_ref[SLOTS + first + h : SLOTS + first + h + 1] = total[:, lanes[h]]


def norm_kernel(hidden_ref, gain_ref, _, scaled_ref, extra_ref):
    widened = hidden_ref[...].astype(F32)
    requests = widened.shape[0]
    scaled_ref[...] = (widened * gain_ref[...].astype(F32).reshape(1, -1)).astype(BF16)
    squares = jnp.sum(widened * widened, axis=1, keepdims=True)
    row = lax.broadcasted_iota(jnp.int32, (requests, LANES), 0)
    lane = lax.broadcasted_iota(jnp.int32, (requests, LANES), 1)
    squares = jnp.sum(jnp.where(row == lane, squares, 0.0), axis=0, keepdims=True)
    first, second, third = split_three(squares)
    upper = jnp.concatenate([first, second], axis=1)
    lower = jnp.concatenate([third, jnp.zeros_like(third)], axis=1)
    place = lax.broadcasted_iota(jnp.int32, extra_ref.shape, 0) - 2 * lax.axis_index("tp")
    extra_ref[...] = jnp.where(place == 0, upper, jnp.where(place == 1, lower, 0.0))


def place():
    rank = lax.axis_index("tp")
    return rank // 4, rank % 2, rank // 2 % 2


def first_kernel(partial_ref, extra_ref, send_ref, keep_ref):
    _, _, near = place()
    rows = partial_ref.shape[1]
    for i in range(2):
        for j in range(2):
            keep_ref[i, j, :rows] = partial_ref[4 * i + 2 * near + j]
            keep_ref[i, j, rows:] = extra_ref[...]
            send_ref[i, j, :rows] = partial_ref[4 * i + 2 * (1 - near) + j].astype(BF16)
            send_ref[i, j, rows:] = extra_ref[...].astype(BF16)


def second_kernel(got_ref, kept_ref, _, send_ref, keep_ref):
    far, _, _ = place()
    keep_ref[...] = kept_ref[far] + got_ref[far].astype(F32)
    send_ref[...] = (kept_ref[1 - far] + got_ref[1 - far].astype(F32)).astype(BF16)


def third_kernel(got_ref, kept_ref, length_ref, frequency_ref, send_ref, last_ref, angle_ref):
    _, side, _ = place()
    last_ref[...] = kept_ref[side] + got_ref[side].astype(F32)
    send_ref[...] = (kept_ref[1 - side] + got_ref[1 - side].astype(F32)).astype(BF16)
    requests, half = angle_ref.shape
    lengths = jnp.broadcast_to(length_ref[...].astype(F32), (LANES, requests)).T
    angle_ref[...] = lengths[:, :half] * frequency_ref[...]


def fresh_kernel(scale, features, got_ref, last_ref, cos_ref, sin_ref, query_ref, kv_ref, score_ref):
    heads, requests, width = query_ref.shape
    total = last_ref[...] + got_ref[...].astype(F32)
    extra = jnp.sum(total[requests:], axis=0, keepdims=True)
    squares = extra[:, :LANES] + extra[:, LANES:]
    row = lax.broadcasted_iota(jnp.int32, (requests, LANES), 0)
    lane = lax.broadcasted_iota(jnp.int32, (requests, LANES), 1)
    squares = jnp.sum(jnp.where(row == lane, squares, 0.0), axis=1, keepdims=True)
    inverse = lax.rsqrt(squares / features + EPSILON)
    projected = total[:requests] * inverse
    key = projected[:, :width]
    key = key * cos_ref[...] + pltpu.roll(key, width // 2, 1) * sin_ref[...]
    key = key.astype(BF16)
    kv_ref[:, :width] = key
    kv_ref[:, width:] = projected[:, width:].astype(BF16)
    key = key.astype(F32)
    scores = jnp.zeros((requests, LANES), F32)
    for h in range(heads):
        score = jnp.sum(query_ref[h].astype(F32) * key, axis=1, keepdims=True)
        scores = jnp.where(lane == h, score * scale, scores)
    score_ref[...] = scores.T[:SLOTS]


def owner_kernel(label_ref, owner_ref):
    slots, requests = owner_ref.shape
    labels = label_ref[...].reshape(slots, LANES)
    owner_ref[...] = jnp.where(
        labels == lax.broadcasted_iota(jnp.int32, (slots, requests), 1), 0.0, FLOOR
    )


def combine_kernel(message_ref, owner_ref, out_ref, stat_ref, fresh_ref, kv_ref, final_hbm, new_kv_hbm, final_ref, sems):
    heads, requests, width = out_ref.shape
    stores = [pltpu.make_async_copy(kv_ref, new_kv_hbm, sems.at[heads])]
    stores[0].start()
    messages = jnp.swapaxes(message_ref[...].astype(F32), 0, 1)
    levels = messages[heads]
    levels = levels[:, :SLOTS] + levels[:, SLOTS : 2 * SLOTS] + levels[:, 2 * SLOTS : 3 * SLOTS]
    owner = owner_ref[...]
    scores = [owner + levels[:, h : h + 1] for h in range(heads)]
    rows = [jnp.max(score, axis=0, keepdims=True) for score in scores]
    moved_best = jnp.concatenate(rows + [rows[0]] * (SLOTS - heads), axis=0)
    stats = stat_ref[...]
    highest = stats[:SLOTS]
    fresh = fresh_ref[...]
    best = jnp.maximum(jnp.maximum(highest, fresh), moved_best)
    weights = [jnp.exp2(scores[h] - best[h : h + 1]) for h in range(heads)]
    rows = [jnp.sum(weight, axis=0, keepdims=True) for weight in weights]
    moved_sums = jnp.concatenate(rows + [rows[0]] * (SLOTS - heads), axis=0)
    factor = jnp.exp2(highest - best)
    fresh = jnp.exp2(fresh - best)
    inverse = 1.0 / (stats[SLOTS:] * factor + fresh + moved_sums)
    columns = jnp.concatenate(
        [factor * inverse, fresh * inverse, jnp.zeros((LANES - 2 * SLOTS, requests), F32)], axis=0
    ).T
    value = kv_ref[:, width:].astype(F32)
    for h in range(heads):
        weight = weights[h] * inverse[h : h + 1]
        coarse = weight.astype(BF16)
        fine = (weight - coarse.astype(F32)).astype(BF16)
        moved = messages[h].astype(BF16)
        total = lax.dot_general(
            jnp.concatenate([coarse, fine], axis=0),
            jnp.concatenate([moved, moved], axis=0),
            TN,
            preferred_element_type=F32,
        )
        total = total + out_ref[h] * columns[:, h : h + 1] + value * columns[:, SLOTS + h : SLOTS + h + 1]
        lanes = pl.ds(h * width, width)
        final_ref[:, h * width : (h + 1) * width] = total.astype(BF16)
        stores.append(pltpu.make_async_copy(final_ref.at[:, lanes], final_hbm.at[:, lanes], sems.at[h]))
        stores[-1].start()
    for store in stores:
        store.wait()


def call(kernel, shapes, ins, scratch=(), limit=8, flops=10**9, moved=0, outs=VMEM):
    return pl.pallas_call(
        kernel,
        out_shape=shapes,
        in_specs=ins,
        out_specs=jax.tree.map(lambda _: outs, shapes),
        scratch_shapes=scratch,
        compiler_params=pltpu.CompilerParams(vmem_limit_bytes=limit * 1024 * 1024),
        cost_estimate=pl.CostEstimate(flops=flops, bytes_accessed=moved, transcendentals=0),
    )


def frequencies(width):
    steps = jnp.arange(width // 2, dtype=F32)
    return (ROPE_BASE ** (-2.0 * steps / width))[None, :]


def body(
    hidden_state,
    norm_gain,
    kv_weight,
    queries,
    pool_keys,
    pool_values,
    page_table,
    lengths,
    move_target,
    move_page,
    move_request,
):
    shape = jax.ShapeDtypeStruct
    requests, heads, width = queries.shape
    pool, _, page_len, _ = pool_keys.shape
    moves = move_page.shape[0]
    instances = lax.axis_size("inst")
    ranks = lax.axis_size("tp")
    features = hidden_state.shape[1] * ranks
    scale = LOG2E / math.sqrt(width)
    root = instances * 26 // 32
    order = [(i + root) % instances for i in range(instances)]

    def exchange(x):
        return lax.all_to_all(x, "inst", 0, 0, tiled=True, axis_index_groups=[order])


    def swap(x, bit):
        return lax.ppermute(x, "tp", [(i, i ^ bit) for i in range(ranks)])

    keys = pool_keys.reshape(pool, page_len, width)
    values = pool_values.reshape(pool, page_len, width)
    by_head = jnp.transpose(queries, (1, 0, 2))

    bits = ((requests - 1).bit_length(), (pool - 1).bit_length())
    plan = (((move_target[:, 0] << bits[0]) | move_request) << bits[1]) | move_page
    labels = call(
        functools.partial(label_kernel, bits, root),
        shape((instances, 1, LANES), jnp.int32),
        [VMEM],
        flops=10**10,
    )(plan.reshape(1, moves))
    labels = exchange(labels)

    scaled, extra = call(
        norm_kernel,
        [shape(hidden_state.shape, BF16), shape((16, 2 * width), F32)],
        [VMEM, VMEM, ANY],
    )(hidden_state, norm_gain, kv_weight)
    partial = jnp.einsum("rf,fgc->grc", scaled, kv_weight, preferred_element_type=F32)
    padded = requests + 16
    send, keep = call(
        first_kernel,
        [shape((2, 2, padded, 2 * width), BF16), shape((2, 2, padded, 2 * width), F32)],
        [VMEM, VMEM],
    )(partial, extra)
    got = swap(send, 2)

    def local(first, stop, cost, *earlier):
        return call(
            functools.partial(local_kernel, scale, first),
            [shape((stop, requests, width), F32), shape((2 * SLOTS, requests), F32)],
            [VMEM] * 5 + [VMEM, VMEM, ANY][: len(earlier)],
            [pltpu.VMEM((pool // 2, 2 * page_len, (stop - first) * requests), F32)],
            limit=16,
            flops=cost,
        )(by_head, keys, values, page_table.T, lengths[None, :], *earlier)

    asked = call(ask_kernel, shape((instances, 2, heads // 2 * width), BF16), [VMEM, VMEM, ANY])(labels, by_head, send)
    asked = exchange(asked)

    out, stats = local(0, heads // 2, 3 * 10**9)
    send, keep = call(
        second_kernel,
        [shape((2, padded, 2 * width), BF16), shape((2, padded, 2 * width), F32)],
        [VMEM, VMEM, ANY],
        flops=SECOND,
    )(got, keep, stats)
    got = swap(send, 4)

    answers = call(
        functools.partial(moved_kernel, scale, heads, bits, root),
        shape((instances, SLOTS, width), BF16),
        [VMEM, VMEM, VMEM, VMEM, ANY],
        [pltpu.VMEM((moves, SLOTS, page_len), F32)],
    )(plan.reshape(1, moves), asked, keys, values, send)
    answers = exchange(answers)

    owner = call(
        owner_kernel, shape((instances, requests), F32), [VMEM], flops=0
    )(labels)
    send, last, angles = call(
        third_kernel,
        [
            shape((padded, 2 * width), BF16),
            shape((padded, 2 * width), F32),
            shape((requests, width // 2), F32),
        ],
        [VMEM] * 4,
        flops=THIRD,
    )(got, keep, lengths[None, :], frequencies(width))
    out, stats = local(heads // 2, heads, LATER, out, stats, send)
    got = swap(send, 1)
    cosine = jnp.cos(angles)
    sine = jnp.sin(angles)
    cosine = jnp.concatenate([cosine, cosine], axis=1)
    sine = jnp.concatenate([-sine, sine], axis=1)
    kv, fresh = call(
        functools.partial(fresh_kernel, scale, features),
        [shape((requests, 2 * width), BF16), shape((SLOTS, requests), F32)],
        [VMEM] * 5,
    )(got, last, cosine, sine, by_head)
    attention_out, new_kv = call(
        combine_kernel,
        [shape((requests, heads * width), BF16), shape((requests, 2 * width), BF16)],
        [VMEM] * 6,
        [pltpu.VMEM((requests, heads * width), BF16), pltpu.SemaphoreType.DMA((heads + 1,))],
        outs=ANY,
    )(answers, owner, out, stats, fresh, kv)
    return (attention_out, new_kv.reshape(requests, 1, 2 * width))


def solution(mesh):
    return jax.shard_map(
        body,
        mesh=mesh,
        in_specs=(
            P("inst", "tp"),
            P("tp"),
            P("tp", None, None),
            P("inst", "tp", None),
            P("inst", "tp", None, None),
            P("inst", "tp", None, None),
            P("inst", None),
            P("inst"),
            P("inst", None),
            P("inst"),
            P("inst"),
        ),
        out_specs=(P("inst", "tp"), P("inst", "tp", None)),
        check_vma=False,
    )
```
